128 devices in a mesh: coil: 4 (over x), frame: 32 (over z, y, core).
Axes of the slice: x: 4, y: 4, z: 4, core: 2. Of those that a mesh axis runs over, the one named last changes fastest.
Arguments:
- image: float32 [128, 32, 2, 32, 128], P(('coil', 'frame')), may hold values from -16 to 16
- sens: bfloat16 [16, 128, 2, 32, 128], P('coil'), may hold values from -3 to 3
- data: bfloat16 [16, 128, 32, 2, 32, 128], P('coil', None, 'frame'), may hold values from -6 to 6
- mask: int32 [32, 32, 128], P('frame'), may hold values 0 or 1
- start: float32 [2, 32, 8], replicated, may hold values from -6 to 6
Outputs:
- new_image: float32 [128, 32, 2, 32, 128], P(('coil', 'frame'))
- spectrum: float32 [8], replicated
The draws below stay inside these ranges and needn't reach their ends.
All inputs are finite; a program needn't handle non-finite values. No bound on the sum of `mask` on one device may be relied on, other than what follows from the above.
Results may differ from the reference program's by a relative error of at most 0.014.
Values may be sent and summed in bfloat16 or wider, within the bound.
No kernel may reach another device: no remote copies, remote signals or barrier semaphores. Data moves between devices by JAX's collectives and lax.ppermute only.
A program may use at most 192 MiB of HBM per device.

```python
import math
import jax
import jax.numpy as jnp
from jax import lax

NX = 128
NY = 128
NZ = 32
COILS = 16
RANK = 8
FRAMES = 32


def draw_image(key, part):
    key = jax.random.fold_in(key, 11)
    first_key, second_key, third_key = jax.random.split(key, 3)
    positions = jnp.arange(NX, dtype=jnp.float32) / (NX - 1)
    common = jax.random.normal(third_key, (NX, 1, 2, NZ, NY), jnp.float32)
    values = jax.random.normal(first_key, (NX, FRAMES, 2, NZ, NY), jnp.float32)
    values = jnp.clip(0.8 * common + 0.6 * values, -4.0, 4.0)
    row_scale = jnp.exp(jnp.log(0.5) + positions * jnp.log(4.0))
    frame_scale = jnp.exp(jax.random.uniform(second_key, (FRAMES,), jnp.float32, -0.69, 0.69))
    return values * row_scale[:, None, None, None, None] * frame_scale[None, :, None, None, None]


def draw_data(key, part):
    key = jax.random.fold_in(key, 23)
    first_key, second_key = jax.random.split(key, 2)
    common = jax.random.normal(first_key, (COILS, NX, 1, 2, NZ, NY), jnp.float32)
    own = jax.random.normal(second_key, (COILS, NX, FRAMES, 2, NZ, NY), jnp.float32)
    values = jnp.clip(0.8 * common + 0.6 * own, -6.0, 6.0)
    return values.astype(jnp.bfloat16)


def with_ends(values, stream_key, low, high):
    dims = values.shape
    index_at = [jax.random.randint(jax.random.fold_in(stream_key, axis), (), 0, dims[axis]) for axis in range(len(dims))]
    values = values.at[tuple(index_at)].set(low)
    longest = dims.index(max(dims))
    index_at[longest] = (index_at[longest] + 1) % dims[longest]
    return values.at[tuple(index_at)].set(high)


def steps_of(rng, dims, shards, low, top_value):
    loudness, own = 1.0, jax.random.fold_in(rng, 6)
    for axis_at, shards_of in shards:
        draws = jnp.exp(jax.random.uniform(jax.random.fold_in(own, axis_at), (shards_of,), jnp.float32, low / len(shards), top_value / len(shards)))
        loudness = loudness * jnp.repeat(draws, dims[axis_at] // shards_of).reshape([-1 if axis == axis_at else 1 for axis in range(len(dims))])
    return loudness


def gaussian(own_key, shape, deviation, most, cuts=(), kind=jnp.bfloat16):
    gain = steps_of(own_key, shape, cuts, -0.22, 0.18) if cuts else 1.0
    array = jax.random.normal(own_key, shape, jnp.float32) * deviation * gain
    return jnp.minimum(jnp.maximum(array, -most), most).astype(kind)


def setup_inputs(seed: int = 0) -> dict:
    seeds = jax.random.split(jax.random.key(seed), 6)
    image = draw_image(jax.random.fold_in(seeds[5], 71), 0)
    sens = gaussian(seeds[1], (COILS, NX, 2, NZ, NY), 0.5, 3.0, ((0, 4),))
    data = draw_data(jax.random.fold_in(seeds[5], 71), 0)
    mask = with_ends((jax.random.randint(seeds[3], (FRAMES, NZ, NY), 0, 4) < 1).astype(jnp.int32), jax.random.fold_in(seeds[3], 1), 0, 1)
    start = gaussian(seeds[4], (2, FRAMES, RANK), 1.0, 6.0, (), jnp.float32)
    return {"image": image, "sens": sens, "data": data, "mask": mask, "start": start}


EPSILON = 1e-06

def dft_tables(length):
    counter = jnp.arange(length, dtype=jnp.int32)
    product = counter[:, None] * counter[None, :] % length
    angles = product.astype(jnp.float32) * (2.0 * math.pi / length)
    factor = 1.0 / math.sqrt(length)
    return ((jnp.cos(angles) * factor).astype(jnp.bfloat16), (jnp.sin(angles) * factor).astype(jnp.bfloat16))

def transform(real_part, imag_part, sign):
    exact_mode = lax.Precision.HIGHEST
    cos_wide, sin_wide = dft_tables(real_part.shape[-1])
    cos_deep, sin_deep = dft_tables(real_part.shape[-2])
    cos_wide = cos_wide.astype(jnp.float32)
    sin_wide = sin_wide.astype(jnp.float32)
    cos_deep = cos_deep.astype(jnp.float32)
    sin_deep = sin_deep.astype(jnp.float32)
    real_f = real_part.astype(jnp.float32)
    imag_f = imag_part.astype(jnp.float32)
    along_real = jnp.einsum('...zy,yk->...zk', real_f, cos_wide, precision=exact_mode) - sign * jnp.einsum('...zy,yk->...zk', imag_f, sin_wide, precision=exact_mode)
    along_imag = jnp.einsum('...zy,yk->...zk', imag_f, cos_wide, precision=exact_mode) + sign * jnp.einsum('...zy,yk->...zk', real_f, sin_wide, precision=exact_mode)
    along_real = along_real.astype(jnp.bfloat16).astype(jnp.float32)
    along_imag = along_imag.astype(jnp.bfloat16).astype(jnp.float32)
    out_real = jnp.einsum('kz,...zy->...ky', cos_deep, along_real, precision=exact_mode) - sign * jnp.einsum('kz,...zy->...ky', sin_deep, along_imag, precision=exact_mode)
    out_imag = jnp.einsum('kz,...zy->...ky', cos_deep, along_imag, precision=exact_mode) + sign * jnp.einsum('kz,...zy->...ky', sin_deep, along_real, precision=exact_mode)
    return (out_real, out_imag)

def frame_gradient(index, image, sens_float, data, mask):
    picture = lax.dynamic_index_in_dim(image, index, 1, keepdims=False)
    pic_real = picture[:, 0][None]
    pic_imag = picture[:, 1][None]
    sens_real = sens_float[:, :, 0]
    sens_imag = sens_float[:, :, 1]
    coil_real = (sens_real * pic_real - sens_imag * pic_imag).astype(jnp.bfloat16)
    coil_imag = (sens_real * pic_imag + sens_imag * pic_real).astype(jnp.bfloat16)
    kspace_real, kspace_imag = transform(coil_real, coil_imag, -1.0)
    measured = lax.dynamic_index_in_dim(data, index, 2, keepdims=False).astype(jnp.float32)
    keep = lax.dynamic_index_in_dim(mask, index, 0, keepdims=False).astype(jnp.float32)[None, None]
    misfit_real = (keep * (kspace_real - measured[:, :, 0])).astype(jnp.bfloat16)
    misfit_imag = (keep * (kspace_imag - measured[:, :, 1])).astype(jnp.bfloat16)
    back_real, back_imag = transform(misfit_real, misfit_imag, 1.0)
    grad_real = lax.optimization_barrier(jnp.sum(sens_real * back_real + sens_imag * back_imag, axis=0))
    grad_imag = lax.optimization_barrier(jnp.sum(sens_real * back_imag - sens_imag * back_real, axis=0))
    return jnp.stack([grad_real, grad_imag], axis=1)

def column_power(block):
    return lax.optimization_barrier(jnp.sum(jnp.real(block) ** 2 + jnp.imag(block) ** 2, axis=0))

def reference(image, sens, data, mask, start):
    exact_mode = lax.Precision.HIGHEST
    sens_float = sens.astype(jnp.float32)
    gradient = lax.map(lambda index: frame_gradient(index, image, sens_float, data, mask), jnp.arange(FRAMES, dtype=jnp.int32))
    casorati = lax.complex(gradient[:, :, 0], gradient[:, :, 1]).reshape(FRAMES, NX * NZ * NY)
    start_complex = lax.complex(start[0], start[1])
    first = jnp.einsum('fv,fk->vk', casorati, start_complex, precision=exact_mode)
    back_first = jnp.einsum('fv,vk->fk', jnp.conj(casorati), first, precision=exact_mode)
    vectors = back_first / jnp.sqrt(column_power(back_first) + EPSILON)[None, :]
    second = jnp.einsum('fv,fk->vk', casorati, vectors, precision=exact_mode)
    back_second = jnp.einsum('fv,vk->fk', jnp.conj(casorati), second, precision=exact_mode)
    second_power = column_power(second)
    spectrum = jnp.sqrt(column_power(back_second) + EPSILON) / jnp.sqrt(second_power + EPSILON)
    total = jnp.sum(second_power)
    update = jnp.einsum('vk,fk->vf', second, jnp.conj(vectors), precision=exact_mode)
    update = jnp.moveaxis(update.reshape(NX, NZ, NY, FRAMES), 3, 1)
    scale = 0.5 * math.sqrt(NX * NY * NZ * FRAMES) / jnp.sqrt(total)
    stacked = jnp.stack([jnp.real(update), jnp.imag(update)], axis=2)
    new_image = 0.5 * image - scale * stacked
    return (new_image, spectrum)
```

```python
import math

import jax
import jax.numpy as jnp
import ml_dtypes
import numpy as np
from jax import lax
from jax.experimental import pallas as pl
from jax.experimental.pallas import tpu as pltpu
from jax.sharding import PartitionSpec as P

NX = 128
NY = 128
NZ = 32
FRAMES = 32
QUARTER = 32
ROWS = 8
EPSILON = 1e-06
BF = jnp.bfloat16
F32 = jnp.float32


def dft_tables(length):
    counter = np.arange(length)
    product = counter[:, None] * counter[None, :] % length
    angles = product.astype(np.float32) * np.float32(2.0 * math.pi / length)
    factor = np.float32(1.0 / math.sqrt(length))
    return np.cos(angles) * factor, np.sin(angles) * factor


def wide_table(sign):
    c, s = dft_tables(NY)
    return np.block([[c, sign * s], [-sign * s, c]]).astype(ml_dtypes.bfloat16)


def deep_table(sign):
    c, s = dft_tables(NZ)
    one = np.block([[c, -sign * s], [sign * s, c]])
    return np.kron(np.eye(4, dtype=np.float32), one).astype(ml_dtypes.bfloat16)


def to_deep(a):
    a = a.reshape(ROWS, NZ, 2 * NY)
    st = jnp.concatenate([a[:, :, :NY], a[:, :, NY:]], axis=1).reshape(2 * ROWS * NZ, NY)
    return jnp.concatenate([st[:256], st[256:]], axis=1)


def from_deep(k):
    k = jnp.concatenate([k[:, :NY], k[:, NY:]], axis=0).reshape(ROWS, 2 * NZ, NY)
    return k[:, :NZ], k[:, NZ:]


def grad_kernel(off_ref, img_ref, sens_ref, data_ref, mask_ref, wf_ref, df_ref, wi_ref, di_ref, out_ref):
    img = img_ref[...].astype(F32)
    x_re, x_im = img[:, :NZ], img[:, NZ:]
    keep = mask_ref[0].astype(F32)[None]
    acc_re = acc_im = None
    for c in range(sens_ref.shape[0]):
        s_re = sens_ref[c, :, 0].astype(F32)
        s_im = sens_ref[c, :, 1].astype(F32)
        u = jnp.concatenate([s_re * x_re - s_im * x_im, s_re * x_im + s_im * x_re], axis=-1)
        u = u.astype(BF).reshape(256, 256)
        a = jnp.dot(u, wf_ref[...], preferred_element_type=F32).astype(BF)
        k_re, k_im = from_deep(jnp.dot(df_ref[...], to_deep(a), preferred_element_type=F32))
        m_re = keep * (k_re - data_ref[c, :, 0, 0].astype(F32))
        m_im = keep * (k_im - data_ref[c, :, 0, 1].astype(F32))
        m = jnp.concatenate([m_re, m_im], axis=-1).astype(BF).reshape(256, 256)
        b = jnp.dot(m, wi_ref[...], preferred_element_type=F32).astype(BF)
        r_re, r_im = from_deep(jnp.dot(di_ref[...], to_deep(b), preferred_element_type=F32))
        g_re = s_re * r_re + s_im * r_im
        g_im = s_re * r_im - s_im * r_re
        acc_re = g_re if acc_re is None else acc_re + g_re
        acc_im = g_im if acc_im is None else acc_im + g_im
    out_ref[...] = jnp.concatenate([acc_re, acc_im], axis=1).astype(BF)


def coil_gradient(img, offset, sens, data, mask):
    n = img.shape[0]
    coils = sens.shape[0]
    return pl.pallas_call(
        grad_kernel,
        grid_spec=pltpu.PrefetchScalarGridSpec(
            num_scalar_prefetch=1,
            grid=(n // ROWS,),
            in_specs=[
                pl.BlockSpec((ROWS, 2 * NZ, NY), lambda i, o: (i, 0, 0)),
                pl.BlockSpec((coils, ROWS, 2, NZ, NY), lambda i, o: (0, o[0] + i, 0, 0, 0)),
                pl.BlockSpec((coils, ROWS, 1, 2, NZ, NY), lambda i, o: (0, o[0] + i, 0, 0, 0, 0)),
                pl.BlockSpec((1, NZ, NY), lambda i, o: (0, 0, 0)),
            ]
            + [pl.BlockSpec((256, 256), lambda i, o: (0, 0))] * 4,
            out_specs=pl.BlockSpec((ROWS, 2 * NZ, NY), lambda i, o: (i, 0, 0)),
        ),
        out_shape=jax.ShapeDtypeStruct((n, 2 * NZ, NY), BF),
        cost_estimate=pl.CostEstimate(
            flops=n * coils * 16 * 2**20, bytes_accessed=n * coils * 40000, transcendentals=0
        ),
        compiler_params=pltpu.CompilerParams(vmem_limit_bytes=32 * 2**20),
        name="coil_gradient",
    )(
        offset, img, sens, data, mask,
        wide_table(-1.0), deep_table(-1.0), wide_table(1.0), deep_table(1.0),
    )


def gram_kernel(g_ref, gt_ref, q_ref, wide):
    wide[...] = g_ref[...].reshape(FRAMES * 2 * NZ, NY).astype(F32)
    total = jnp.zeros((2 * FRAMES, 2 * FRAMES), F32)
    for z in range(0, NZ, 2):
        pair = []
        for d in (z, z + 1):
            re = wide[pl.ds(d, FRAMES, stride=2 * NZ), :]
            im = wide[pl.ds(NZ + d, FRAMES, stride=2 * NZ), :]
            block = jnp.concatenate([re, im], axis=0).astype(BF)
            gt_ref[d] = block
            pair.append(block)
        both = jnp.concatenate(pair, axis=1)
        total += lax.dot_general(both, both, (((1,), (1,)), ((), ())), preferred_element_type=F32)
    h_re = total[:FRAMES, :FRAMES] + total[FRAMES:, FRAMES:]
    h_im = total[:FRAMES, FRAMES:] - total[FRAMES:, :FRAMES]
    row = lax.broadcasted_iota(jnp.int32, (FRAMES, FRAMES), 0)
    col = lax.broadcasted_iota(jnp.int32, (FRAMES, FRAMES), 1)
    q = jnp.where(row <= col, h_re, h_im)
    q_ref[...] = jnp.concatenate([q[8 * j : 8 * j + 8] for j in range(4)], axis=1)


def gram(g):
    return pl.pallas_call(
        gram_kernel,
        out_shape=(
            jax.ShapeDtypeStruct((NZ, 2 * FRAMES, NY), BF),
            jax.ShapeDtypeStruct((8, 128), F32),
        ),
        scratch_shapes=[pltpu.VMEM((FRAMES * 2 * NZ, NY), F32)],
        compiler_params=pltpu.CompilerParams(vmem_limit_bytes=32 * 2**20),
        name="gram",
    )(g)


def exact(a, b, dims=((1,), (0,))):
    return lax.dot_general(
        a, b, (dims, ((), ())), precision=lax.Precision.HIGHEST, preferred_element_type=F32
    )


def final_kernel(q0, q1, q2, q3, start_ref, gt_ref, image_ref, out_ref, spec_ref, wide):
    packed = (q0[...] + q1[...]) + (q2[...] + q3[...])
    q = jnp.concatenate([packed[:, 32 * j : 32 * j + 32] for j in range(4)], axis=0)
    qt = q.T
    row = lax.broadcasted_iota(jnp.int32, (FRAMES, FRAMES), 0)
    col = lax.broadcasted_iota(jnp.int32, (FRAMES, FRAMES), 1)
    h_re = jnp.where(row <= col, q, qt)
    h_im = jnp.where(row > col, q, jnp.where(row < col, -qt, 0.0))
    v_re, v_im = start_ref[0], start_ref[1]
    w_re = exact(h_re, v_re) - exact(h_im, v_im)
    w_im = exact(h_re, v_im) + exact(h_im, v_re)
    length = jnp.sqrt(jnp.sum(w_re * w_re + w_im * w_im, axis=0, keepdims=True) + EPSILON)
    v_re, v_im = w_re / length, w_im / length
    w_re = exact(h_re, v_re) - exact(h_im, v_im)
    w_im = exact(h_re, v_im) + exact(h_im, v_re)
    power = jnp.maximum(jnp.sum(v_re * w_re + v_im * w_im, axis=0, keepdims=True), 0.0)
    last = jnp.sum(w_re * w_re + w_im * w_im, axis=0, keepdims=True)
    spec_ref[...] = jnp.sqrt(last + EPSILON) / jnp.sqrt(power + EPSILON)
    total = jnp.sum(power, axis=1, keepdims=True)
    scale = 0.5 * math.sqrt(NX * NY * NZ * FRAMES) / jnp.sqrt(total)
    lanes = ((1,), (1,))
    t_re = (exact(v_re, v_re, lanes) + exact(v_im, v_im, lanes)) * scale
    t_im = (exact(v_im, v_re, lanes) - exact(v_re, v_im, lanes)) * scale
    left = jnp.concatenate(
        [jnp.concatenate([t_re, t_im], axis=1), jnp.concatenate([-t_im, t_re], axis=1)], axis=0
    )
    high = left.astype(BF)
    low = (left - high.astype(F32)).astype(BF)
    left = jnp.concatenate([high, low], axis=1)
    for z in range(NZ):
        block = gt_ref[z]
        update = jnp.dot(left, jnp.concatenate([block, block], axis=0), preferred_element_type=F32)
        wide[pl.ds(z, FRAMES, stride=2 * NZ), :] = update[:FRAMES]
        wide[pl.ds(NZ + z, FRAMES, stride=2 * NZ), :] = update[FRAMES:]
    out_ref[...] = 0.5 * image_ref[...] - wide[...].reshape(FRAMES, 2 * NZ, NY)


def finish(parts, start, gt, image):
    return pl.pallas_call(
        final_kernel,
        out_shape=(
            jax.ShapeDtypeStruct((FRAMES, 2 * NZ, NY), F32),
            jax.ShapeDtypeStruct((1, start.shape[2]), F32),
        ),
        scratch_shapes=[pltpu.VMEM((FRAMES * 2 * NZ, NY), F32)],
        compiler_params=pltpu.CompilerParams(vmem_limit_bytes=32 * 2**20),
        name="finish",
    )(*parts, start, gt, image)


RIGHT = [(i, (i + 1) % 4) for i in range(4)]
LEFT = [(i, (i + 3) % 4) for i in range(4)]


def local(image, sens, data, mask, start):
    flat = image.reshape(FRAMES, 2 * NZ, NY)
    coil = lax.axis_index("coil")

    def partial(img, distance, skip=0):
        offset = ((coil + distance) % 4) * (QUARTER // ROWS) + skip // ROWS
        return coil_gradient(img, offset.astype(jnp.int32).reshape(1), sens, data, mask)

    half = QUARTER // 2
    own = lax.all_to_all(flat.astype(BF), "frame", split_axis=0, concat_axis=0, tiled=True)
    from_left = lax.ppermute(own, "coil", RIGHT)
    from_right = lax.ppermute(own, "coil", LEFT)
    far_low = lax.ppermute(from_left[:half], "coil", RIGHT)
    far_high = lax.ppermute(from_right[half:], "coil", LEFT)
    part_own = partial(own, 0)
    part_left = partial(from_left, 3)
    part_right = partial(from_right, 1)
    part_low = partial(far_low, 2)
    part_high = partial(far_high, 2, half)
    low = lax.ppermute(part_low, "coil", RIGHT)
    high = lax.ppermute(part_high, "coil", LEFT)

    def add(a, b):
        return (a.astype(F32) + b.astype(F32)).astype(BF)

    to_right = jnp.concatenate([add(part_right[:half], low), part_right[half:]])
    to_left = jnp.concatenate([part_left[:half], add(part_left[half:], high)])
    in_left = lax.ppermute(to_right, "coil", RIGHT)
    in_right = lax.ppermute(to_left, "coil", LEFT)
    gradient = (part_own.astype(F32) + in_left.astype(F32) + in_right.astype(F32)).astype(BF)
    frames = lax.all_to_all(gradient, "frame", split_axis=0, concat_axis=0, tiled=True)
    gt, q = gram(frames)
    spread = lax.all_to_all(
        jnp.broadcast_to(q[None], (FRAMES, 8, 128)), "frame", split_axis=0, concat_axis=0, tiled=True
    )
    q = jnp.sum(spread, axis=0)
    parts = [q] + [lax.ppermute(q, "coil", [(i, i ^ d) for i in range(4)]) for d in (1, 2, 3)]
    new_image, spectrum = finish(parts, start, gt, flat)
    return new_image.reshape(image.shape), spectrum[0]


def solution(mesh):
    return jax.shard_map(
        local,
        mesh=mesh,
        in_specs=(
            P(("coil", "frame"), None, None, None, None),
            P("coil", None, None, None, None),
            P("coil", None, "frame", None, None, None),
            P("frame", None, None),
            P(),
        ),
        out_specs=(P(("coil", "frame"), None, None, None, None), P()),
        check_vma=False,
    )
```

```python
import math

import jax
import jax.numpy as jnp
import ml_dtypes
import numpy as np
from jax import lax
from jax.experimental import pallas as pl
from jax.experimental.pallas import tpu as pltpu
from jax.sharding import PartitionSpec as P

NX = 128
NY = 128
NZ = 32
FRAMES = 32
HALF = 16
EPSILON = 1e-06
BF = jnp.bfloat16
F32 = jnp.float32


def dft_tables(length):
    counter = np.arange(length)
    product = counter[:, None] * counter[None, :] % length
    angles = product.astype(np.float32) * np.float32(2.0 * math.pi / length)
    factor = np.float32(1.0 / math.sqrt(length))
    return np.cos(angles) * factor, np.sin(angles) * factor


def wide_table(sign):
    c, s = dft_tables(NY)
    return np.block([[c, sign * s], [-sign * s, c]]).astype(ml_dtypes.bfloat16)


def deep_table(sign):
    c, s = dft_tables(NZ)
    one = np.block([[c, -sign * s], [sign * s, c]])
    return np.kron(np.eye(4, dtype=np.float32), one).astype(ml_dtypes.bfloat16)


def to_deep(a):
    out = []
    for j in range(0, a.shape[0], 256):
        one = a[j : j + 256].reshape(8, NZ, 2 * NY)
        one = jnp.concatenate([one[:, :, :NY], one[:, :, NY:]], axis=1).reshape(512, NY)
        out += [one[:256], one[256:]]
    return jnp.concatenate(out, axis=1)


def from_deep(k):
    k = jnp.concatenate([k[:, j : j + NY] for j in range(0, k.shape[1], NY)], axis=0)
    k = k.reshape(-1, 2 * NZ, NY)
    return k[:, :NZ], k[:, NZ:]


def grad_kernel(coil_ref, *refs):
    images, refs = refs[:2], refs[2:]
    sens_ref, data_ref, mask_ref, wf_ref, df_ref, wi_ref, di_ref = refs[:7]
    outs = refs[7:]
    step = pl.program_id(0)
    coils = sens_ref.shape[0]
    span = HALF * NZ
    img = jnp.where(step == 0, images[0][...], images[1][...]).astype(F32)
    x_re, x_im = img[:, :NZ], img[:, NZ:]
    keep = mask_ref[0].astype(F32)[None]

    def sens(c):
        return sens_ref[c, :, 0].astype(F32), sens_ref[c, :, 1].astype(F32)

    def join(re, im):
        return jnp.concatenate([re, im], axis=-1).astype(BF).reshape(span, 2 * NY)

    u = []
    for c in range(coils):
        s_re, s_im = sens(c)
        u.append(join(s_re * x_re - s_im * x_im, s_re * x_im + s_im * x_re))
    a = jnp.dot(jnp.concatenate(u, axis=0), wf_ref[...], preferred_element_type=F32).astype(BF)
    k = jnp.dot(df_ref[...], to_deep(a), preferred_element_type=F32)
    m = []
    for c in range(coils):
        k_re, k_im = from_deep(k[:, span * c : span * (c + 1)])
        k_re = keep * (k_re - data_ref[c, :, 0, 0].astype(F32))
        k_im = keep * (k_im - data_ref[c, :, 0, 1].astype(F32))
        m.append(join(k_re, k_im))
    b = jnp.dot(jnp.concatenate(m, axis=0), wi_ref[...], preferred_element_type=F32).astype(BF)
    r = jnp.dot(di_ref[...], to_deep(b), preferred_element_type=F32)
    acc_re = acc_im = 0.0
    for c in range(coils):
        s_re, s_im = sens(c)
        r_re, r_im = from_deep(r[:, span * c : span * (c + 1)])
        acc_re += s_re * r_re + s_im * r_im
        acc_im += s_re * r_im - s_im * r_re
    total = jnp.concatenate([acc_re, acc_im], axis=1).astype(BF)
    for j in range(2):

        @pl.when(step == j)
        def _(j=j):
            outs[j][...] = total


def coil_gradient(images, places, coil, sens, data, mask):
    coils = sens.shape[0]
    rows = (HALF, 2 * NZ, NY)
    (far, low), (far_next, low_next) = places

    def place(i, coil):
        return ((coil[0] + far + i * (far_next - far)) & 3) * 2 + low + i * (low_next - low)

    return pl.pallas_call(
        grad_kernel,
        grid_spec=pltpu.PrefetchScalarGridSpec(
            num_scalar_prefetch=1,
            grid=(2,),
            in_specs=[pl.BlockSpec(rows, lambda i, o, block=block: (block, 0, 0)) for _, block in images]
            + [
                pl.BlockSpec((coils, HALF, 2, NZ, NY), lambda i, o: (0, place(i, o), 0, 0, 0)),
                pl.BlockSpec((coils, HALF, 1, 2, NZ, NY), lambda i, o: (0, place(i, o), 0, 0, 0, 0)),
                pl.BlockSpec((1, NZ, NY), lambda i, o: (0, 0, 0)),
            ]
            + [pl.BlockSpec((256, 256), lambda i, o: (0, 0))] * 4,
            out_specs=[pl.BlockSpec(rows, lambda i, o: (0, 0, 0))] * 2,
        ),
        out_shape=[jax.ShapeDtypeStruct(rows, BF)] * 2,
        cost_estimate=pl.CostEstimate(
            flops=2 * HALF * coils * 32 * 2**20,
            bytes_accessed=2 * HALF * coils * 40000,
            transcendentals=0,
        ),
        compiler_params=pltpu.CompilerParams(vmem_limit_bytes=57 * 2**20),
        name="coil_gradient",
    )(
        coil, images[0][0], images[1][0], sens, data, mask,
        wide_table(-1.0), deep_table(-1.0), wide_table(1.0), deep_table(1.0),
    )


def sums_kernel(a0, b0, c0, a1, b1, c1, out_ref):
    out_ref[:HALF] = (a0[...].astype(F32) + b0[...].astype(F32) + c0[...].astype(F32)).astype(BF)
    out_ref[HALF:] = (a1[...].astype(F32) + b1[...].astype(F32) + c1[...].astype(F32)).astype(BF)


def join_sums(first, second):
    return pl.pallas_call(
        sums_kernel,
        out_shape=jax.ShapeDtypeStruct((2 * HALF, 2 * NZ, NY), BF),
        name="join_sums",
    )(*first, *second)


def gram_kernel(g_ref, gt_ref, q_ref, wide):
    wide[...] = g_ref[...].reshape(FRAMES * 2 * NZ, NY).astype(F32)
    total = jnp.zeros((2 * FRAMES, 2 * FRAMES), F32)
    for z in range(0, NZ, 2):
        pair = []
        for d in (z, z + 1):
            re = wide[pl.ds(d, FRAMES, stride=2 * NZ), :]
            im = wide[pl.ds(NZ + d, FRAMES, stride=2 * NZ), :]
            block = jnp.concatenate([re, im], axis=0).astype(BF)
            gt_ref[d] = block
            pair.append(block)
        both = jnp.concatenate(pair, axis=1)
        total += lax.dot_general(both, both, (((1,), (1,)), ((), ())), preferred_element_type=F32)
    h_re = total[:FRAMES, :FRAMES] + total[FRAMES:, FRAMES:]
    h_im = total[:FRAMES, FRAMES:] - total[FRAMES:, :FRAMES]
    row = lax.broadcasted_iota(jnp.int32, (FRAMES, FRAMES), 0)
    col = lax.broadcasted_iota(jnp.int32, (FRAMES, FRAMES), 1)
    q = jnp.where(row <= col, h_re, h_im)
    q_ref[...] = jnp.concatenate([q[8 * j : 8 * j + 8] for j in range(4)], axis=1)


def gram(g):
    return pl.pallas_call(
        gram_kernel,
        out_shape=(
            jax.ShapeDtypeStruct((NZ, 2 * FRAMES, NY), BF),
            jax.ShapeDtypeStruct((8, 128), F32),
        ),
        scratch_shapes=[pltpu.VMEM((FRAMES * 2 * NZ, NY), F32)],
        compiler_params=pltpu.CompilerParams(vmem_limit_bytes=32 * 2**20),
        name="gram",
    )(g)


def exact(a, b, dims=((1,), (0,))):
    return lax.dot_general(
        a, b, (dims, ((), ())), precision=lax.Precision.HIGHEST, preferred_element_type=F32
    )


def final_kernel(q0, q1, q2, q3, start_ref, gt_ref, image_ref, out_ref, spec_ref, wide):
    packed = (q0[...] + q1[...]) + (q2[...] + q3[...])
    q = jnp.concatenate([packed[:, 32 * j : 32 * j + 32] for j in range(4)], axis=0)
    qt = q.T
    row = lax.broadcasted_iota(jnp.int32, (FRAMES, FRAMES), 0)
    col = lax.broadcasted_iota(jnp.int32, (FRAMES, FRAMES), 1)
    h_re = jnp.where(row <= col, q, qt)
    h_im = jnp.where(row > col, q, jnp.where(row < col, -qt, 0.0))
    v_re, v_im = start_ref[0], start_ref[1]
    w_re = exact(h_re, v_re) - exact(h_im, v_im)
    w_im = exact(h_re, v_im) + exact(h_im, v_re)
    length = jnp.sqrt(jnp.sum(w_re * w_re + w_im * w_im, axis=0, keepdims=True) + EPSILON)
    v_re, v_im = w_re / length, w_im / length
    w_re = exact(h_re, v_re) - exact(h_im, v_im)
    w_im = exact(h_re, v_im) + exact(h_im, v_re)
    power = jnp.maximum(jnp.sum(v_re * w_re + v_im * w_im, axis=0, keepdims=True), 0.0)
    last = jnp.sum(w_re * w_re + w_im * w_im, axis=0, keepdims=True)
    spec_ref[...] = jnp.sqrt(last + EPSILON) / jnp.sqrt(power + EPSILON)
    total = jnp.sum(power, axis=1, keepdims=True)
    scale = 0.5 * math.sqrt(NX * NY * NZ * FRAMES) / jnp.sqrt(total)
    lanes = ((1,), (1,))
    t_re = (exact(v_re, v_re, lanes) + exact(v_im, v_im, lanes)) * scale
    t_im = (exact(v_im, v_re, lanes) - exact(v_re, v_im, lanes)) * scale
    left = jnp.concatenate(
        [jnp.concatenate([t_re, t_im], axis=1), jnp.concatenate([-t_im, t_re], axis=1)], axis=0
    )
    high = left.astype(BF)
    low = (left - high.astype(F32)).astype(BF)
    left = jnp.concatenate([high, low], axis=1)
    for z in range(NZ):
        block = gt_ref[z]
        update = jnp.dot(left, jnp.concatenate([block, block], axis=0), preferred_element_type=F32)
        wide[pl.ds(z, FRAMES, stride=2 * NZ), :] = update[:FRAMES]
        wide[pl.ds(NZ + z, FRAMES, stride=2 * NZ), :] = update[FRAMES:]
    out_ref[...] = 0.5 * image_ref[...] - wide[...].reshape(FRAMES, 2 * NZ, NY)


def finish(parts, start, gt, image):
    return pl.pallas_call(
        final_kernel,
        out_shape=(
            jax.ShapeDtypeStruct((FRAMES, 2 * NZ, NY), F32),
            jax.ShapeDtypeStruct((1, start.shape[2]), F32),
        ),
        scratch_shapes=[pltpu.VMEM((FRAMES * 2 * NZ, NY), F32)],
        compiler_params=pltpu.CompilerParams(vmem_limit_bytes=32 * 2**20),
        name="finish",
    )(*parts, start, gt, image)


RIGHT = [(i, (i + 1) % 4) for i in range(4)]
LEFT = [(i, (i + 3) % 4) for i in range(4)]


def after(x, *others):
    return lax.optimization_barrier((x,) + others)[0]


def local(image, sens, data, mask, start):
    flat = image.reshape(FRAMES, 2 * NZ, NY)
    coil = lax.axis_index("coil").astype(jnp.int32).reshape(1)

    def partial(images, places, *others):
        return coil_gradient(images, places, after(coil, *others), sens, data, mask)

    def right(x):
        return lax.ppermute(x, "coil", RIGHT)

    def left(x):
        return lax.ppermute(x, "coil", LEFT)

    def add(*terms):
        return sum(t.astype(F32) for t in terms).astype(BF)

    own = lax.all_to_all(flat.astype(BF), "frame", split_axis=0, concat_axis=0, tiled=True)
    own0, own1 = own[:HALF], own[HALF:]
    left0, right1 = right(own0), left(own1)
    g_own = partial([(own, 0), (own, 1)], [(0, 0), (0, 1)])
    left0, right1 = after(left0, g_own[0], right1), after(right1, g_own[0], left0)
    far0, far1 = right(left0), left(right1)
    g_left0, g_right1 = partial([(left0, 0), (right1, 0)], [(3, 0), (1, 1)])
    left1, right0 = right(after(own1, g_left0)), left(after(own0, g_left0))
    g_far0, g_far1 = partial([(far0, 0), (far1, 0)], [(2, 0), (2, 1)], g_left0)
    low, high = right(g_far0), left(g_far1)
    in_left1, in_right0 = right(after(g_right1, g_far0)), left(after(g_left0, g_far0))
    g_left1, g_right0 = partial([(left1, 0), (right0, 0)], [(3, 1), (1, 0)], g_far0)
    in_left0, in_right1 = right(add(g_right0, low)), left(add(g_left1, high))
    gradient = join_sums((g_own[0], in_left0, in_right0), (g_own[1], in_left1, in_right1))
    frames = lax.all_to_all(gradient, "frame", split_axis=0, concat_axis=0, tiled=True)
    gt, q = gram(frames)
    spread = lax.all_to_all(
        jnp.broadcast_to(q[None], (FRAMES, 8, 128)), "frame", split_axis=0, concat_axis=0, tiled=True
    )
    q = jnp.sum(spread, axis=0)
    parts = [q] + [lax.ppermute(q, "coil", [(i, i ^ d) for i in range(4)]) for d in (1, 2, 3)]
    new_image, spectrum = finish(parts, start, gt, flat)
    return new_image.reshape(image.shape), spectrum[0]


def solution(mesh):
    return jax.shard_map(
        local,
        mesh=mesh,
        in_specs=(
            P(("coil", "frame"), None, None, None, None),
            P("coil", None, None, None, None),
            P("coil", None, "frame", None, None, None),
            P("frame", None, None),
            P(),
        ),
        out_specs=(P(("coil", "frame"), None, None, None, None), P()),
        check_vma=False,
    )
```

```python
import math

import jax
import jax.numpy as jnp
import ml_dtypes
import numpy as np
from jax import lax
from jax.experimental import pallas as pl
from jax.experimental.pallas import tpu as pltpu
from jax.sharding import PartitionSpec as P

NX = 128
NY = 128
NZ = 32
FRAMES = 32
HALF = 16
EPSILON = 1e-06
BF = jnp.bfloat16
F32 = jnp.float32


def dft_tables(length):
    counter = np.arange(length)
    product = counter[:, None] * counter[None, :] % length
    angles = product.astype(np.float32) * np.float32(2.0 * math.pi / length)
    factor = np.float32(1.0 / math.sqrt(length))
    return np.cos(angles) * factor, np.sin(angles) * factor


def wide_table(sign):
    c, s = dft_tables(NY)
    return np.block([[c, sign * s], [-sign * s, c]]).astype(ml_dtypes.bfloat16)


def deep_table(sign):
    c, s = dft_tables(NZ)
    one = np.block([[c, -sign * s], [sign * s, c]])
    return np.kron(np.eye(4, dtype=np.float32), one).astype(ml_dtypes.bfloat16)


def to_deep(a):
    out = []
    for j in range(0, a.shape[0], 256):
        one = a[j : j + 256].reshape(8, NZ, 2 * NY)
        one = jnp.concatenate([one[:, :, :NY], one[:, :, NY:]], axis=1).reshape(512, NY)
        out += [one[:256], one[256:]]
    return jnp.concatenate(out, axis=1)


def from_deep(k):
    k = jnp.concatenate([k[:, j : j + NY] for j in range(0, k.shape[1], NY)], axis=0)
    k = k.reshape(-1, 2 * NZ, NY)
    return k[:, :NZ], k[:, NZ:]


def grad_kernel(coil_ref, *refs):
    steps = (len(refs) - 7) // 2
    images, refs = refs[:steps], refs[steps:]
    sens_ref, data_ref, mask_ref, wf_ref, df_ref, wi_ref, di_ref = refs[:7]
    outs = refs[7:]
    step = pl.program_id(0)
    coils = sens_ref.shape[0]
    span = HALF * NZ
    img = images[0][...]
    if steps == 2:
        img = jnp.where(step == 0, img, images[1][...])
    img = img.astype(F32)
    x_re, x_im = img[:, :NZ], img[:, NZ:]
    keep = mask_ref[0].astype(F32)[None]

    def sens(c):
        return sens_ref[c, :, 0].astype(F32), sens_ref[c, :, 1].astype(F32)

    def join(re, im):
        return jnp.concatenate([re, im], axis=-1).astype(BF).reshape(span, 2 * NY)

    u = []
    for c in range(coils):
        s_re, s_im = sens(c)
        u.append(join(s_re * x_re - s_im * x_im, s_re * x_im + s_im * x_re))
    a = jnp.dot(jnp.concatenate(u, axis=0), wf_ref[...], preferred_element_type=F32).astype(BF)
    k = jnp.dot(df_ref[...], to_deep(a), preferred_element_type=F32)
    m = []
    for c in range(coils):
        k_re, k_im = from_deep(k[:, span * c : span * (c + 1)])
        k_re = keep * (k_re - data_ref[c, :, 0, 0].astype(F32))
        k_im = keep * (k_im - data_ref[c, :, 0, 1].astype(F32))
        m.append(join(k_re, k_im))
    b = jnp.dot(jnp.concatenate(m, axis=0), wi_ref[...], preferred_element_type=F32).astype(BF)
    r = jnp.dot(di_ref[...], to_deep(b), preferred_element_type=F32)
    acc_re = acc_im = 0.0
    for c in range(coils):
        s_re, s_im = sens(c)
        r_re, r_im = from_deep(r[:, span * c : span * (c + 1)])
        acc_re += s_re * r_re + s_im * r_im
        acc_im += s_re * r_im - s_im * r_re
    total = jnp.concatenate([acc_re, acc_im], axis=1).astype(BF)
    for j in range(steps):

        @pl.when(step == j)
        def _(j=j):
            outs[j][...] = total


def coil_gradient(images, places, coil, sens, data, mask, room):
    coils = sens.shape[0]
    rows = (HALF, 2 * NZ, NY)
    steps = len(images)
    (far, low), (far_next, low_next) = places[0], places[-1]

    def place(i, coil):
        return ((coil[0] + far + i * (far_next - far)) & 3) * 2 + low + i * (low_next - low)

    return pl.pallas_call(
        grad_kernel,
        grid_spec=pltpu.PrefetchScalarGridSpec(
            num_scalar_prefetch=1,
            grid=(steps,),
            in_specs=[pl.BlockSpec(rows, lambda i, o, block=block: (block, 0, 0)) for _, block in images]
            + [
                pl.BlockSpec((coils, HALF, 2, NZ, NY), lambda i, o: (0, place(i, o), 0, 0, 0)),
                pl.BlockSpec((coils, HALF, 1, 2, NZ, NY), lambda i, o: (0, place(i, o), 0, 0, 0, 0)),
                pl.BlockSpec((1, NZ, NY), lambda i, o: (0, 0, 0)),
            ]
            + [pl.BlockSpec((256, 256), lambda i, o: (0, 0))] * 4,
            out_specs=[pl.BlockSpec(rows, lambda i, o: (0, 0, 0))] * steps,
        ),
        out_shape=[jax.ShapeDtypeStruct(rows, BF)] * steps,
        cost_estimate=pl.CostEstimate(
            flops=steps * HALF * coils * 32 * 2**20,
            bytes_accessed=steps * HALF * coils * 40000,
            transcendentals=0,
        ),
        compiler_params=pltpu.CompilerParams(vmem_limit_bytes=room * 2**20),
        name="coil_gradient",
    )(
        coil, *(x for x, _ in images), sens, data, mask,
        wide_table(-1.0), deep_table(-1.0), wide_table(1.0), deep_table(1.0),
    )


SMALL = pltpu.CompilerParams(vmem_limit_bytes=8 * 2**20)


def total_of(refs):
    return sum(ref[...].astype(F32) for ref in refs).astype(BF)


def pair_kernel(a0, b0, a1, b1, out0, out1):
    out0[...] = total_of((a0, b0))
    out1[...] = total_of((a1, b1))


def pair_sums(first, second):
    return pl.pallas_call(
        pair_kernel, out_shape=[jax.ShapeDtypeStruct((HALF, 2 * NZ, NY), BF)] * 2,
        compiler_params=SMALL, name="pair_sums",
    )(*first, *second)


def join_kernel(a0, b0, c0, a1, b1, c1, out_ref):
    out_ref[:HALF] = total_of((a0, b0, c0))
    out_ref[HALF:] = total_of((a1, b1, c1))


def join_sums(first, second):
    return pl.pallas_call(
        join_kernel, out_shape=jax.ShapeDtypeStruct((2 * HALF, 2 * NZ, NY), BF),
        compiler_params=SMALL, name="join_sums",
    )(*first, *second)


def gram_kernel(g_ref, gt_ref, q_ref, wide):
    wide[...] = g_ref[...].reshape(FRAMES * 2 * NZ, NY).astype(F32)
    total = jnp.zeros((2 * FRAMES, 2 * FRAMES), F32)
    for z in range(0, NZ, 2):
        pair = []
        for d in (z, z + 1):
            re = wide[pl.ds(d, FRAMES, stride=2 * NZ), :]
            im = wide[pl.ds(NZ + d, FRAMES, stride=2 * NZ), :]
            block = jnp.concatenate([re, im], axis=0).astype(BF)
            gt_ref[d] = block
            pair.append(block)
        both = jnp.concatenate(pair, axis=1)
        total += lax.dot_general(both, both, (((1,), (1,)), ((), ())), preferred_element_type=F32)
    h_re = total[:FRAMES, :FRAMES] + total[FRAMES:, FRAMES:]
    h_im = total[:FRAMES, FRAMES:] - total[FRAMES:, :FRAMES]
    row = lax.broadcasted_iota(jnp.int32, (FRAMES, FRAMES), 0)
    col = lax.broadcasted_iota(jnp.int32, (FRAMES, FRAMES), 1)
    q = jnp.where(row <= col, h_re, h_im)
    q_ref[...] = jnp.concatenate([q[8 * j : 8 * j + 8] for j in range(4)], axis=1)


def gram(g):
    return pl.pallas_call(
        gram_kernel,
        out_shape=(
            jax.ShapeDtypeStruct((NZ, 2 * FRAMES, NY), BF),
            jax.ShapeDtypeStruct((8, 128), F32),
        ),
        scratch_shapes=[pltpu.VMEM((FRAMES * 2 * NZ, NY), F32)],
        compiler_params=pltpu.CompilerParams(vmem_limit_bytes=32 * 2**20),
        name="gram",
    )(g)


def exact(a, b, dims=((1,), (0,))):
    return lax.dot_general(
        a, b, (dims, ((), ())), precision=lax.Precision.HIGHEST, preferred_element_type=F32
    )


def final_kernel(q0, q1, q2, q3, start_ref, gt_ref, image_ref, out_ref, spec_ref, wide):
    packed = (q0[...] + q1[...]) + (q2[...] + q3[...])
    q = jnp.concatenate([packed[:, 32 * j : 32 * j + 32] for j in range(4)], axis=0)
    qt = q.T
    row = lax.broadcasted_iota(jnp.int32, (FRAMES, FRAMES), 0)
    col = lax.broadcasted_iota(jnp.int32, (FRAMES, FRAMES), 1)
    h_re = jnp.where(row <= col, q, qt)
    h_im = jnp.where(row > col, q, jnp.where(row < col, -qt, 0.0))
    v_re, v_im = start_ref[0], start_ref[1]
    w_re = exact(h_re, v_re) - exact(h_im, v_im)
    w_im = exact(h_re, v_im) + exact(h_im, v_re)
    length = jnp.sqrt(jnp.sum(w_re * w_re + w_im * w_im, axis=0, keepdims=True) + EPSILON)
    v_re, v_im = w_re / length, w_im / length
    w_re = exact(h_re, v_re) - exact(h_im, v_im)
    w_im = exact(h_re, v_im) + exact(h_im, v_re)
    power = jnp.maximum(jnp.sum(v_re * w_re + v_im * w_im, axis=0, keepdims=True), 0.0)
    last = jnp.sum(w_re * w_re + w_im * w_im, axis=0, keepdims=True)
    spec_ref[...] = jnp.sqrt(last + EPSILON) / jnp.sqrt(power + EPSILON)
    total = jnp.sum(power, axis=1, keepdims=True)
    scale = 0.5 * math.sqrt(NX * NY * NZ * FRAMES) / jnp.sqrt(total)
    lanes = ((1,), (1,))
    t_re = (exact(v_re, v_re, lanes) + exact(v_im, v_im, lanes)) * scale
    t_im = (exact(v_im, v_re, lanes) - exact(v_re, v_im, lanes)) * scale
    left = jnp.concatenate(
        [jnp.concatenate([t_re, t_im], axis=1), jnp.concatenate([-t_im, t_re], axis=1)], axis=0
    )
    high = left.astype(BF)
    low = (left - high.astype(F32)).astype(BF)
    left = jnp.concatenate([high, low], axis=1)
    for z in range(NZ):
        block = gt_ref[z]
        update = jnp.dot(left, jnp.concatenate([block, block], axis=0), preferred_element_type=F32)
        wide[pl.ds(z, FRAMES, stride=2 * NZ), :] = update[:FRAMES]
        wide[pl.ds(NZ + z, FRAMES, stride=2 * NZ), :] = update[FRAMES:]
    out_ref[...] = 0.5 * image_ref[...] - wide[...].reshape(FRAMES, 2 * NZ, NY)


def finish(parts, start, gt, image):
    return pl.pallas_call(
        final_kernel,
        out_shape=(
            jax.ShapeDtypeStruct((FRAMES, 2 * NZ, NY), F32),
            jax.ShapeDtypeStruct((1, start.shape[2]), F32),
        ),
        scratch_shapes=[pltpu.VMEM((FRAMES * 2 * NZ, NY), F32)],
        compiler_params=pltpu.CompilerParams(vmem_limit_bytes=32 * 2**20),
        name="finish",
    )(*parts, start, gt, image)


RIGHT = [(i, (i + 1) % 4) for i in range(4)]
LEFT = [(i, (i + 3) % 4) for i in range(4)]


def after(x, *others):
    return lax.optimization_barrier((x,) + others)[0]


def local(image, sens, data, mask, start):
    flat = image.reshape(FRAMES, 2 * NZ, NY)
    coil = lax.axis_index("coil").astype(jnp.int32).reshape(1)

    def partial(images, places, *others, room=50):
        return coil_gradient(images, places, after(coil, *others), sens, data, mask, room)

    def right(x):
        return lax.ppermute(x, "coil", RIGHT)

    def left(x):
        return lax.ppermute(x, "coil", LEFT)

    own = lax.all_to_all(flat.astype(BF), "frame", split_axis=0, concat_axis=0, tiled=True)
    own0, own1 = own[:HALF], own[HALF:]
    left0, right1 = right(own0), left(own1)
    (g_own0,) = partial([(own, 0)], [(0, 0)], room=57)
    left1, right0 = right(after(own1, g_own0)), left(after(own0, g_own0))
    (g_own1,) = partial([(own, 1)], [(0, 1)], g_own0, room=57)
    left0, right1 = after(left0, g_own1, right1), after(right1, g_own1, left0)
    far0, far1 = right(left0), left(right1)
    g_left0, g_right1 = partial([(left0, 0), (right1, 0)], [(3, 0), (1, 1)])
    in_left1, in_right0 = right(g_right1), left(g_left0)
    g_far0, g_far1 = partial([(far0, 0), (far1, 0)], [(2, 0), (2, 1)], g_left0)
    low, high = right(g_far0), left(g_far1)
    g_left1, g_right0 = partial([(left1, 0), (right0, 0)], [(3, 1), (1, 0)], g_far0)
    to_right, to_left = pair_sums((g_right0, low), (g_left1, high))
    in_left0, in_right1 = right(to_right), left(to_left)
    gradient = join_sums((g_own0, in_left0, in_right0), (g_own1, in_left1, in_right1))
    frames = lax.all_to_all(gradient, "frame", split_axis=0, concat_axis=0, tiled=True)
    gt, q = gram(frames)
    spread = lax.all_to_all(
        jnp.broadcast_to(q[None], (FRAMES, 8, 128)), "frame", split_axis=0, concat_axis=0, tiled=True
    )
    q = jnp.sum(spread, axis=0)
    parts = [q] + [lax.ppermute(q, "coil", [(i, i ^ d) for i in range(4)]) for d in (1, 2, 3)]
    new_image, spectrum = finish(parts, start, gt, flat)
    return new_image.reshape(image.shape), spectrum[0]


def solution(mesh):
    return jax.shard_map(
        local,
        mesh=mesh,
        in_specs=(
            P(("coil", "frame"), None, None, None, None),
            P("coil", None, None, None, None),
            P("coil", None, "frame", None, None, None),
            P("frame", None, None),
            P(),
        ),
        out_specs=(P(("coil", "frame"), None, None, None, None), P()),
        check_vma=False,
    )
```

```python
import math

import jax
import jax.numpy as jnp
import ml_dtypes
import numpy as np
from jax import lax
from jax.experimental import pallas as pl
from jax.experimental.pallas import tpu as pltpu
from jax.sharding import PartitionSpec as P

NX = 128
NY = 128
NZ = 32
FRAMES = 32
HALF = 16
EPSILON = 1e-06
BF = jnp.bfloat16
F32 = jnp.float32


def dft_tables(length):
    counter = np.arange(length)
    product = counter[:, None] * counter[None, :] % length
    angles = product.astype(np.float32) * np.float32(2.0 * math.pi / length)
    factor = np.float32(1.0 / math.sqrt(length))
    return np.cos(angles) * factor, np.sin(angles) * factor


def wide_table(sign):
    c, s = dft_tables(NY)
    return np.block([[c, sign * s], [-sign * s, c]]).astype(ml_dtypes.bfloat16)


def deep_table(sign):
    c, s = dft_tables(NZ)
    one = np.block([[c, -sign * s], [sign * s, c]])
    return np.kron(np.eye(4, dtype=np.float32), one).astype(ml_dtypes.bfloat16)


def to_deep(a):
    out = []
    for j in range(0, a.shape[0], 256):
        one = a[j : j + 256].reshape(8, NZ, 2 * NY)
        one = jnp.concatenate([one[:, :, :NY], one[:, :, NY:]], axis=1).reshape(512, NY)
        out += [one[:256], one[256:]]
    return jnp.concatenate(out, axis=1)


def from_deep(k):
    k = jnp.concatenate([k[:, j : j + NY] for j in range(0, k.shape[1], NY)], axis=0)
    k = k.reshape(-1, 2 * NZ, NY)
    return k[:, :NZ], k[:, NZ:]


def grad_kernel(coil_ref, *refs):
    steps = (len(refs) - 4) // 2
    images, refs = refs[:steps], refs[steps:]
    sens_ref, data_ref, mask_ref, tables = refs[:4]
    outs = refs[4:]
    step = pl.program_id(0)
    coils = sens_ref.shape[0]
    span = HALF * NZ
    img = images[0][...]
    if steps == 2:
        img = jnp.where(step == 0, img, images[1][...])
    img = img.astype(F32)
    x_re, x_im = img[:, :NZ], img[:, NZ:]
    keep = mask_ref[0].astype(F32)[None]

    def sens(c):
        return sens_ref[c, :, 0].astype(F32), sens_ref[c, :, 1].astype(F32)

    def join(re, im):
        return jnp.concatenate([re, im], axis=-1).astype(BF).reshape(span, 2 * NY)

    u = []
    for c in range(coils):
        s_re, s_im = sens(c)
        u.append(join(s_re * x_re - s_im * x_im, s_re * x_im + s_im * x_re))
    a = jnp.dot(jnp.concatenate(u, axis=0), tables[0], preferred_element_type=F32).astype(BF)
    k = jnp.dot(tables[1], to_deep(a), preferred_element_type=F32)
    m = []
    for c in range(coils):
        k_re, k_im = from_deep(k[:, span * c : span * (c + 1)])
        k_re = keep * (k_re - data_ref[c, :, 0, 0].astype(F32))
        k_im = keep * (k_im - data_ref[c, :, 0, 1].astype(F32))
        m.append(join(k_re, k_im))
    b = jnp.dot(jnp.concatenate(m, axis=0), tables[2], preferred_element_type=F32).astype(BF)
    r = jnp.dot(tables[3], to_deep(b), preferred_element_type=F32)
    acc_re = acc_im = 0.0
    for c in range(coils):
        s_re, s_im = sens(c)
        r_re, r_im = from_deep(r[:, span * c : span * (c + 1)])
        acc_re += s_re * r_re + s_im * r_im
        acc_im += s_re * r_im - s_im * r_re
    total = jnp.concatenate([acc_re, acc_im], axis=1).astype(BF)
    for j in range(steps):

        @pl.when(step == j)
        def _(j=j):
            outs[j][...] = total


def coil_gradient(images, places, coil, sens, data, mask, room, weight=1):
    coils = sens.shape[0]
    rows = (HALF, 2 * NZ, NY)
    steps = len(images)
    (far, low), (far_next, low_next) = places[0], places[-1]

    def place(i, coil):
        return ((coil[0] + far + i * (far_next - far)) & 3) * 2 + low + i * (low_next - low)

    return pl.pallas_call(
        grad_kernel,
        grid_spec=pltpu.PrefetchScalarGridSpec(
            num_scalar_prefetch=1,
            grid=(steps,),
            in_specs=[pl.BlockSpec(rows, lambda i, o, block=block: (block, 0, 0)) for _, block in images]
            + [
                pl.BlockSpec((coils, HALF, 2, NZ, NY), lambda i, o: (0, place(i, o), 0, 0, 0)),
                pl.BlockSpec((coils, HALF, 1, 2, NZ, NY), lambda i, o: (0, place(i, o), 0, 0, 0, 0)),
                pl.BlockSpec((1, NZ, NY), lambda i, o: (0, 0, 0)),
            ]
            + [pl.BlockSpec((4, 256, 256), lambda i, o: (0, 0, 0))],
            out_specs=[pl.BlockSpec(rows, lambda i, o: (0, 0, 0))] * steps,
        ),
        out_shape=[jax.ShapeDtypeStruct(rows, BF)] * steps,
        cost_estimate=pl.CostEstimate(
            flops=weight * steps * HALF * coils * 32 * 2**20,
            bytes_accessed=steps * HALF * coils * 40000,
            transcendentals=0,
        ),
        compiler_params=pltpu.CompilerParams(vmem_limit_bytes=room * 2**20),
        name="coil_gradient",
    )(
        coil, *(x for x, _ in images), sens, data, mask,
        np.stack([wide_table(-1.0), deep_table(-1.0), wide_table(1.0), deep_table(1.0)]),
    )


SMALL = pltpu.CompilerParams(vmem_limit_bytes=8 * 2**20)


def total_of(refs):
    return sum(ref[...].astype(F32) for ref in refs).astype(BF)


def pair_kernel(a0, b0, a1, b1, out0, out1):
    out0[...] = total_of((a0, b0))
    out1[...] = total_of((a1, b1))


def pair_sums(first, second):
    return pl.pallas_call(
        pair_kernel, out_shape=[jax.ShapeDtypeStruct((HALF, 2 * NZ, NY), BF)] * 2,
        compiler_params=SMALL, name="pair_sums",
    )(*first, *second)


def join_kernel(a0, b0, c0, a1, b1, c1, out_ref):
    out_ref[:HALF] = total_of((a0, b0, c0))
    out_ref[HALF:] = total_of((a1, b1, c1))


def join_sums(first, second):
    return pl.pallas_call(
        join_kernel, out_shape=jax.ShapeDtypeStruct((2 * HALF, 2 * NZ, NY), BF),
        compiler_params=SMALL, name="join_sums",
    )(*first, *second)


def gram_kernel(g_ref, gt_ref, q_ref, wide):
    wide[...] = g_ref[...].reshape(FRAMES * 2 * NZ, NY).astype(F32)
    total = jnp.zeros((2 * FRAMES, 2 * FRAMES), F32)
    for z in range(0, NZ, 2):
        pair = []
        for d in (z, z + 1):
            re = wide[pl.ds(d, FRAMES, stride=2 * NZ), :]
            im = wide[pl.ds(NZ + d, FRAMES, stride=2 * NZ), :]
            block = jnp.concatenate([re, im], axis=0).astype(BF)
            gt_ref[d] = block
            pair.append(block)
        both = jnp.concatenate(pair, axis=1)
        total += lax.dot_general(both, both, (((1,), (1,)), ((), ())), preferred_element_type=F32)
    h_re = total[:FRAMES, :FRAMES] + total[FRAMES:, FRAMES:]
    h_im = total[:FRAMES, FRAMES:] - total[FRAMES:, :FRAMES]
    row = lax.broadcasted_iota(jnp.int32, (FRAMES, FRAMES), 0)
    col = lax.broadcasted_iota(jnp.int32, (FRAMES, FRAMES), 1)
    q = jnp.where(row <= col, h_re, h_im)
    q_ref[...] = jnp.concatenate([q[8 * j : 8 * j + 8] for j in range(4)], axis=1)


def gram(g):
    return pl.pallas_call(
        gram_kernel,
        out_shape=(
            jax.ShapeDtypeStruct((NZ, 2 * FRAMES, NY), BF),
            jax.ShapeDtypeStruct((8, 128), F32),
        ),
        scratch_shapes=[pltpu.VMEM((FRAMES * 2 * NZ, NY), F32)],
        compiler_params=pltpu.CompilerParams(vmem_limit_bytes=32 * 2**20),
        name="gram",
    )(g)


def exact(a, b, dims=((1,), (0,))):
    return lax.dot_general(
        a, b, (dims, ((), ())), precision=lax.Precision.HIGHEST, preferred_element_type=F32
    )


def final_kernel(q0, q1, q2, q3, start_ref, gt_ref, image_ref, out_ref, spec_ref, wide):
    packed = (q0[...] + q1[...]) + (q2[...] + q3[...])
    q = jnp.concatenate([packed[:, 32 * j : 32 * j + 32] for j in range(4)], axis=0)
    qt = q.T
    row = lax.broadcasted_iota(jnp.int32, (FRAMES, FRAMES), 0)
    col = lax.broadcasted_iota(jnp.int32, (FRAMES, FRAMES), 1)
    h_re = jnp.where(row <= col, q, qt)
    h_im = jnp.where(row > col, q, jnp.where(row < col, -qt, 0.0))
    v_re, v_im = start_ref[0], start_ref[1]
    w_re = exact(h_re, v_re) - exact(h_im, v_im)
    w_im = exact(h_re, v_im) + exact(h_im, v_re)
    length = jnp.sqrt(jnp.sum(w_re * w_re + w_im * w_im, axis=0, keepdims=True) + EPSILON)
    v_re, v_im = w_re / length, w_im / length
    w_re = exact(h_re, v_re) - exact(h_im, v_im)
    w_im = exact(h_re, v_im) + exact(h_im, v_re)
    power = jnp.maximum(jnp.sum(v_re * w_re + v_im * w_im, axis=0, keepdims=True), 0.0)
    last = jnp.sum(w_re * w_re + w_im * w_im, axis=0, keepdims=True)
    spec_ref[...] = jnp.sqrt(last + EPSILON) / jnp.sqrt(power + EPSILON)
    total = jnp.sum(power, axis=1, keepdims=True)
    scale = 0.5 * math.sqrt(NX * NY * NZ * FRAMES) / jnp.sqrt(total)
    lanes = ((1,), (1,))
    t_re = (exact(v_re, v_re, lanes) + exact(v_im, v_im, lanes)) * scale
    t_im = (exact(v_im, v_re, lanes) - exact(v_re, v_im, lanes)) * scale
    left = jnp.concatenate(
        [jnp.concatenate([t_re, t_im], axis=1), jnp.concatenate([-t_im, t_re], axis=1)], axis=0
    )
    high = left.astype(BF)
    low = (left - high.astype(F32)).astype(BF)
    left = jnp.concatenate([high, low], axis=1)
    for z in range(NZ):
        block = gt_ref[z]
        update = jnp.dot(left, jnp.concatenate([block, block], axis=0), preferred_element_type=F32)
        wide[pl.ds(z, FRAMES, stride=2 * NZ), :] = update[:FRAMES]
        wide[pl.ds(NZ + z, FRAMES, stride=2 * NZ), :] = update[FRAMES:]
    out_ref[...] = 0.5 * image_ref[...] - wide[...].reshape(FRAMES, 2 * NZ, NY)


def finish(parts, start, gt, image):
    return pl.pallas_call(
        final_kernel,
        out_shape=(
            jax.ShapeDtypeStruct((FRAMES, 2 * NZ, NY), F32),
            jax.ShapeDtypeStruct((1, start.shape[2]), F32),
        ),
        scratch_shapes=[pltpu.VMEM((FRAMES * 2 * NZ, NY), F32)],
        compiler_params=pltpu.CompilerParams(vmem_limit_bytes=32 * 2**20),
        name="finish",
    )(*parts, start, gt, image)


RIGHT = [(i, (i + 1) % 4) for i in range(4)]
LEFT = [(i, (i + 3) % 4) for i in range(4)]


def after(x, *others):
    return lax.optimization_barrier((x,) + others)[0]


def local(image, sens, data, mask, start):
    flat = image.reshape(FRAMES, 2 * NZ, NY)
    coil = lax.axis_index("coil").astype(jnp.int32).reshape(1)

    def partial(images, places, *others, room=28):
        return coil_gradient(images, places, after(coil, *others), sens, data, mask, room)

    def right(x):
        return lax.ppermute(x, "coil", RIGHT)

    def left(x):
        return lax.ppermute(x, "coil", LEFT)

    own = lax.all_to_all(flat.astype(BF), "frame", split_axis=0, concat_axis=0, tiled=True)
    own0, own1 = own[:HALF], own[HALF:]
    left0, right1 = right(own0), left(own1)
    rows = [lax.dynamic_slice_in_dim(x, coil[0] * 2 * HALF, 2 * HALF, axis=1) for x in (sens, data)]
    g_own0, g_own1 = coil_gradient(
        [(own, 0), (own, 1)], [(0, 0), (0, 1)], jnp.zeros_like(coil), *rows, mask, 28, 2
    )
    left0, right1 = after(left0, g_own1, right1), after(right1, g_own1, left0)
    far0, far1 = right(left0), left(right1)
    g_left0, g_right1 = partial([(left0, 0), (right1, 0)], [(3, 0), (1, 1)])
    left1, right0 = right(after(own1, g_left0)), left(after(own0, g_left0))
    g_far0, g_far1 = partial([(far0, 0), (far1, 0)], [(2, 0), (2, 1)], g_left0)
    low, high = right(g_far0), left(g_far1)
    in_left1, in_right0 = right(after(g_right1, g_far0)), left(after(g_left0, g_far0))
    g_left1, g_right0 = partial([(left1, 0), (right0, 0)], [(3, 1), (1, 0)], g_far0)
    to_right, to_left = pair_sums((g_right0, low), (g_left1, high))
    in_left0, in_right1 = right(to_right), left(to_left)
    gradient = join_sums((g_own0, in_left0, in_right0), (g_own1, in_left1, in_right1))
    frames = lax.all_to_all(gradient, "frame", split_axis=0, concat_axis=0, tiled=True)
    gt, q = gram(frames)
    spread = lax.all_to_all(
        jnp.broadcast_to(q[None], (FRAMES, 8, 128)), "frame", split_axis=0, concat_axis=0, tiled=True
    )
    q = jnp.sum(spread, axis=0)
    parts = [q] + [lax.ppermute(q, "coil", [(i, i ^ d) for i in range(4)]) for d in (1, 2, 3)]
    new_image, spectrum = finish(parts, start, gt, flat)
    return new_image.reshape(image.shape), spectrum[0]


def solution(mesh):
    return jax.shard_map(
        local,
        mesh=mesh,
        in_specs=(
            P(("coil", "frame"), None, None, None, None),
            P("coil", None, None, None, None),
            P("coil", None, "frame", None, None, None),
            P("frame", None, None),
            P(),
        ),
        out_specs=(P(("coil", "frame"), None, None, None, None), P()),
        check_vma=False,
    )
```

```python
import math

import jax
import jax.numpy as jnp
import ml_dtypes
import numpy as np
from jax import lax
from jax.experimental import pallas as pl
from jax.experimental.pallas import tpu as pltpu
from jax.sharding import PartitionSpec as P

NX = 128
NY = 128
NZ = 32
FRAMES = 32
HALF = 16
EPSILON = 1e-06
BF = jnp.bfloat16
F32 = jnp.float32


def dft_tables(length):
    counter = np.arange(length)
    product = counter[:, None] * counter[None, :] % length
    angles = product.astype(np.float32) * np.float32(2.0 * math.pi / length)
    factor = np.float32(1.0 / math.sqrt(length))
    return np.cos(angles) * factor, np.sin(angles) * factor


def wide_table(sign):
    c, s = dft_tables(NY)
    return np.block([[c, sign * s], [-sign * s, c]]).astype(ml_dtypes.bfloat16)


def deep_table(sign):
    c, s = dft_tables(NZ)
    one = np.block([[c, -sign * s], [sign * s, c]])
    return np.kron(np.eye(4, dtype=np.float32), one).astype(ml_dtypes.bfloat16)


def to_deep(a):
    out = []
    for j in range(0, a.shape[0], 256):
        one = a[j : j + 256].reshape(8, NZ, 2 * NY)
        one = jnp.concatenate([one[:, :, :NY], one[:, :, NY:]], axis=1).reshape(512, NY)
        out += [one[:256], one[256:]]
    return jnp.concatenate(out, axis=1)


def from_deep(k):
    k = jnp.concatenate([k[:, j : j + NY] for j in range(0, k.shape[1], NY)], axis=0)
    k = k.reshape(-1, 2 * NZ, NY)
    return k[:, :NZ], k[:, NZ:]


def grad_kernel(coil_ref, *refs):
    steps = (len(refs) - 4) // 2
    images, refs = refs[:steps], refs[steps:]
    sens_ref, data_ref, mask_ref, tables = refs[:4]
    outs = refs[4:]
    step = pl.program_id(0)
    coils = sens_ref.shape[0]
    span = HALF * NZ
    img = images[0][...]
    if steps == 2:
        img = jnp.where(step == 0, img, images[1][...])
    img = img.astype(F32)
    x_re, x_im = img[:, :NZ], img[:, NZ:]
    keep = mask_ref[0].astype(F32)[None]

    def sens(c):
        return sens_ref[c, :, 0].astype(F32), sens_ref[c, :, 1].astype(F32)

    def join(re, im):
        return jnp.concatenate([re, im], axis=-1).astype(BF).reshape(span, 2 * NY)

    u = []
    for c in range(coils):
        s_re, s_im = sens(c)
        u.append(join(s_re * x_re - s_im * x_im, s_re * x_im + s_im * x_re))
    a = jnp.dot(jnp.concatenate(u, axis=0), tables[0], preferred_element_type=F32).astype(BF)
    k = jnp.dot(tables[1], to_deep(a), preferred_element_type=F32)
    m = []
    for c in range(coils):
        k_re, k_im = from_deep(k[:, span * c : span * (c + 1)])
        k_re = keep * (k_re - data_ref[c, :, 0, 0].astype(F32))
        k_im = keep * (k_im - data_ref[c, :, 0, 1].astype(F32))
        m.append(join(k_re, k_im))
    b = jnp.dot(jnp.concatenate(m, axis=0), tables[2], preferred_element_type=F32).astype(BF)
    r = jnp.dot(tables[3], to_deep(b), preferred_element_type=F32)
    acc_re = acc_im = 0.0
    for c in range(coils):
        s_re, s_im = sens(c)
        r_re, r_im = from_deep(r[:, span * c : span * (c + 1)])
        acc_re += s_re * r_re + s_im * r_im
        acc_im += s_re * r_im - s_im * r_re
    total = jnp.concatenate([acc_re, acc_im], axis=1).astype(BF)
    for j in range(steps):

        @pl.when(step == j)
        def _(j=j):
            outs[j][...] = total


def coil_gradient(images, places, coil, sens, data, mask, room, weight=1):
    coils = sens.shape[0]
    rows = (HALF, 2 * NZ, NY)
    steps = len(images)
    (far, low), (far_next, low_next) = places[0], places[-1]

    def place(i, coil):
        return ((coil[0] + far + i * (far_next - far)) & 3) * 2 + low + i * (low_next - low)

    return pl.pallas_call(
        grad_kernel,
        grid_spec=pltpu.PrefetchScalarGridSpec(
            num_scalar_prefetch=1,
            grid=(steps,),
            in_specs=[pl.BlockSpec(rows, lambda i, o, block=block: (block, 0, 0)) for _, block in images]
            + [
                pl.BlockSpec((coils, HALF, 2, NZ, NY), lambda i, o: (0, place(i, o), 0, 0, 0)),
                pl.BlockSpec((coils, HALF, 1, 2, NZ, NY), lambda i, o: (0, place(i, o), 0, 0, 0, 0)),
                pl.BlockSpec((1, NZ, NY), lambda i, o: (0, 0, 0)),
            ]
            + [pl.BlockSpec((4, 256, 256), lambda i, o: (0, 0, 0))],
            out_specs=[pl.BlockSpec(rows, lambda i, o: (0, 0, 0))] * steps,
        ),
        out_shape=[jax.ShapeDtypeStruct(rows, BF)] * steps,
        cost_estimate=pl.CostEstimate(
            flops=weight * steps * HALF * coils * 32 * 2**20,
            bytes_accessed=steps * HALF * coils * 40000,
            transcendentals=0,
        ),
        compiler_params=pltpu.CompilerParams(vmem_limit_bytes=room * 2**20),
        name="coil_gradient",
    )(
        coil, *(x for x, _ in images), sens, data, mask,
        np.stack([wide_table(-1.0), deep_table(-1.0), wide_table(1.0), deep_table(1.0)]),
    )


SMALL = pltpu.CompilerParams(vmem_limit_bytes=8 * 2**20)


def total_of(refs):
    return sum(ref[...].astype(F32) for ref in refs).astype(BF)


def pair_kernel(a, b, out):
    out[...] = total_of((a, b))


def pair_sum(a, b):
    return pl.pallas_call(
        pair_kernel, out_shape=jax.ShapeDtypeStruct(a.shape, BF), compiler_params=SMALL, name="pair_sum",
    )(a, b)


def join_kernel(a0, b0, c0, a1, b1, c1, out_ref):
    out_ref[:HALF] = total_of((a0, b0, c0))
    out_ref[HALF:] = total_of((a1, b1, c1))


def join_sums(first, second):
    return pl.pallas_call(
        join_kernel, out_shape=jax.ShapeDtypeStruct((2 * HALF, 2 * NZ, NY), BF),
        compiler_params=SMALL, name="join_sums",
    )(*first, *second)


def gram_kernel(g_ref, gt_ref, q_ref, wide):
    wide[...] = g_ref[...].reshape(FRAMES * 2 * NZ, NY).astype(F32)
    total = jnp.zeros((2 * FRAMES, 2 * FRAMES), F32)
    for z in range(0, NZ, 2):
        pair = []
        for d in (z, z + 1):
            re = wide[pl.ds(d, FRAMES, stride=2 * NZ), :]
            im = wide[pl.ds(NZ + d, FRAMES, stride=2 * NZ), :]
            block = jnp.concatenate([re, im], axis=0).astype(BF)
            gt_ref[d] = block
            pair.append(block)
        both = jnp.concatenate(pair, axis=1)
        total += lax.dot_general(both, both, (((1,), (1,)), ((), ())), preferred_element_type=F32)
    h_re = total[:FRAMES, :FRAMES] + total[FRAMES:, FRAMES:]
    h_im = total[:FRAMES, FRAMES:] - total[FRAMES:, :FRAMES]
    row = lax.broadcasted_iota(jnp.int32, (FRAMES, FRAMES), 0)
    col = lax.broadcasted_iota(jnp.int32, (FRAMES, FRAMES), 1)
    q = jnp.where(row <= col, h_re, h_im)
    q_ref[...] = jnp.concatenate([q[8 * j : 8 * j + 8] for j in range(4)], axis=1)


def gram(g):
    return pl.pallas_call(
        gram_kernel,
        out_shape=(
            jax.ShapeDtypeStruct((NZ, 2 * FRAMES, NY), BF),
            jax.ShapeDtypeStruct((8, 128), F32),
        ),
        scratch_shapes=[pltpu.VMEM((FRAMES * 2 * NZ, NY), F32)],
        compiler_params=pltpu.CompilerParams(vmem_limit_bytes=32 * 2**20),
        name="gram",
    )(g)


def exact(a, b, dims=((1,), (0,))):
    return lax.dot_general(
        a, b, (dims, ((), ())), precision=lax.Precision.HIGHEST, preferred_element_type=F32
    )


def final_kernel(q0, q1, q2, q3, start_ref, gt_ref, image_ref, out_ref, spec_ref, wide):
    packed = (q0[...] + q1[...]) + (q2[...] + q3[...])
    q = jnp.concatenate([packed[:, 32 * j : 32 * j + 32] for j in range(4)], axis=0)
    qt = q.T
    row = lax.broadcasted_iota(jnp.int32, (FRAMES, FRAMES), 0)
    col = lax.broadcasted_iota(jnp.int32, (FRAMES, FRAMES), 1)
    h_re = jnp.where(row <= col, q, qt)
    h_im = jnp.where(row > col, q, jnp.where(row < col, -qt, 0.0))
    v_re, v_im = start_ref[0], start_ref[1]
    w_re = exact(h_re, v_re) - exact(h_im, v_im)
    w_im = exact(h_re, v_im) + exact(h_im, v_re)
    length = jnp.sqrt(jnp.sum(w_re * w_re + w_im * w_im, axis=0, keepdims=True) + EPSILON)
    v_re, v_im = w_re / length, w_im / length
    w_re = exact(h_re, v_re) - exact(h_im, v_im)
    w_im = exact(h_re, v_im) + exact(h_im, v_re)
    power = jnp.maximum(jnp.sum(v_re * w_re + v_im * w_im, axis=0, keepdims=True), 0.0)
    last = jnp.sum(w_re * w_re + w_im * w_im, axis=0, keepdims=True)
    spec_ref[...] = jnp.sqrt(last + EPSILON) / jnp.sqrt(power + EPSILON)
    total = jnp.sum(power, axis=1, keepdims=True)
    scale = 0.5 * math.sqrt(NX * NY * NZ * FRAMES) / jnp.sqrt(total)
    lanes = ((1,), (1,))
    t_re = (exact(v_re, v_re, lanes) + exact(v_im, v_im, lanes)) * scale
    t_im = (exact(v_im, v_re, lanes) - exact(v_re, v_im, lanes)) * scale
    left = jnp.concatenate(
        [jnp.concatenate([t_re, t_im], axis=1), jnp.concatenate([-t_im, t_re], axis=1)], axis=0
    )
    high = left.astype(BF)
    low = (left - high.astype(F32)).astype(BF)
    left = jnp.concatenate([high, low], axis=1)
    for z in range(NZ):
        block = gt_ref[z]
        update = jnp.dot(left, jnp.concatenate([block, block], axis=0), preferred_element_type=F32)
        wide[pl.ds(z, FRAMES, stride=2 * NZ), :] = update[:FRAMES]
        wide[pl.ds(NZ + z, FRAMES, stride=2 * NZ), :] = update[FRAMES:]
    out_ref[...] = 0.5 * image_ref[...] - wide[...].reshape(FRAMES, 2 * NZ, NY)


def finish(parts, start, gt, image):
    return pl.pallas_call(
        final_kernel,
        out_shape=(
            jax.ShapeDtypeStruct((FRAMES, 2 * NZ, NY), F32),
            jax.ShapeDtypeStruct((1, start.shape[2]), F32),
        ),
        scratch_shapes=[pltpu.VMEM((FRAMES * 2 * NZ, NY), F32)],
        compiler_params=pltpu.CompilerParams(vmem_limit_bytes=32 * 2**20),
        name="finish",
    )(*parts, start, gt, image)


RIGHT = [(i, (i + 1) % 4) for i in range(4)]
LEFT = [(i, (i + 3) % 4) for i in range(4)]


def after(x, *others):
    return lax.optimization_barrier((x,) + others)[0]


def local(image, sens, data, mask, start):
    flat = image.reshape(FRAMES, 2 * NZ, NY)
    coil = lax.axis_index("coil").astype(jnp.int32).reshape(1)

    def partial(images, places, *others, room=28):
        return coil_gradient(images, places, after(coil, *others), sens, data, mask, room)

    def right(x):
        return lax.ppermute(x, "coil", RIGHT)

    def left(x):
        return lax.ppermute(x, "coil", LEFT)

    own = lax.all_to_all(flat.astype(BF), "frame", split_axis=0, concat_axis=0, tiled=True)
    own0, own1 = own[:HALF], own[HALF:]
    left0, right1 = right(own0), left(own1)
    rows = [lax.dynamic_slice_in_dim(x, coil[0] * 2 * HALF, 2 * HALF, axis=1) for x in (sens, data)]
    g_own0, g_own1 = coil_gradient(
        [(own, 0), (own, 1)], [(0, 0), (0, 1)], jnp.zeros_like(coil), *rows, mask, 28, 2
    )
    left0, right1 = after(left0, g_own1, right1), after(right1, g_own1, left0)
    far0, far1 = right(left0), left(right1)
    g_left0, g_right1 = partial([(left0, 0), (right1, 0)], [(3, 0), (1, 1)])
    left1, right0 = right(after(own1, g_left0)), left(after(own0, g_left0))
    (g_far0,) = partial([(far0, 0)], [(2, 0)], g_left0)
    (g_far1,) = partial([(far1, 0)], [(2, 1)], g_far0)
    low, high = right(g_far0), left(g_far1)
    in_left1, in_right0 = right(after(g_right1, g_far1)), left(after(g_left0, g_far1))
    g_left1, g_right0 = partial([(left1, 0), (right0, 0)], [(3, 1), (1, 0)], g_far1)
    in_left0, in_right1 = right(pair_sum(g_right0, low)), left(pair_sum(g_left1, high))
    gradient = join_sums((g_own0, in_left0, in_right0), (g_own1, in_left1, in_right1))
    frames = lax.all_to_all(gradient, "frame", split_axis=0, concat_axis=0, tiled=True)
    gt, q = gram(frames)
    spread = lax.all_to_all(
        jnp.broadcast_to(q[None], (FRAMES, 8, 128)), "frame", split_axis=0, concat_axis=0, tiled=True
    )
    q = jnp.sum(spread, axis=0)
    parts = [q] + [lax.ppermute(q, "coil", [(i, i ^ d) for i in range(4)]) for d in (1, 2, 3)]
    new_image, spectrum = finish(parts, start, gt, flat)
    return new_image.reshape(image.shape), spectrum[0]


def solution(mesh):
    return jax.shard_map(
        local,
        mesh=mesh,
        in_specs=(
            P(("coil", "frame"), None, None, None, None),
            P("coil", None, None, None, None),
            P("coil", None, "frame", None, None, None),
            P("frame", None, None),
            P(),
        ),
        out_specs=(P(("coil", "frame"), None, None, None, None), P()),
        check_vma=False,
    )
```

```python
import math

import jax
import jax.numpy as jnp
import ml_dtypes
import numpy as np
from jax import lax
from jax.experimental import pallas as pl
from jax.experimental.pallas import tpu as pltpu
from jax.sharding import PartitionSpec as P

NX = 128
NY = 128
NZ = 32
FRAMES = 32
HALF = 16
EPSILON = 1e-06
BF = jnp.bfloat16
F32 = jnp.float32


def dft_tables(length):
    counter = np.arange(length)
    product = counter[:, None] * counter[None, :] % length
    angles = product.astype(np.float32) * np.float32(2.0 * math.pi / length)
    factor = np.float32(1.0 / math.sqrt(length))
    return np.cos(angles) * factor, np.sin(angles) * factor


def wide_table(sign):
    c, s = dft_tables(NY)
    return np.block([[c, sign * s], [-sign * s, c]]).astype(ml_dtypes.bfloat16)


def deep_table(sign):
    c, s = dft_tables(NZ)
    one = np.block([[c, -sign * s], [sign * s, c]])
    return np.kron(np.eye(4, dtype=np.float32), one).astype(ml_dtypes.bfloat16)


def to_deep(a):
    out = []
    for j in range(0, a.shape[0], 256):
        one = a[j : j + 256].reshape(8, NZ, 2 * NY)
        one = jnp.concatenate([one[:, :, :NY], one[:, :, NY:]], axis=1).reshape(512, NY)
        out += [one[:256], one[256:]]
    return jnp.concatenate(out, axis=1)


def from_deep(k):
    k = jnp.concatenate([k[:, j : j + NY] for j in range(0, k.shape[1], NY)], axis=0)
    k = k.reshape(-1, 2 * NZ, NY)
    return k[:, :NZ], k[:, NZ:]


def grad_kernel(coil_ref, *refs):
    steps = (len(refs) - 4) // 2
    images, refs = refs[:steps], refs[steps:]
    sens_ref, data_ref, mask_ref, tables = refs[:4]
    outs = refs[4:]
    step = pl.program_id(0)
    coils = sens_ref.shape[0]
    span = HALF * NZ
    img = images[0][...]
    if steps == 2:
        img = jnp.where(step == 0, img, images[1][...])
    img = img.astype(F32)
    x_re, x_im = img[:, :NZ], img[:, NZ:]
    keep = mask_ref[0].astype(F32)[None]

    def sens(c):
        return sens_ref[c, :, 0].astype(F32), sens_ref[c, :, 1].astype(F32)

    def join(re, im):
        return jnp.concatenate([re, im], axis=-1).astype(BF).reshape(span, 2 * NY)

    u = []
    for c in range(coils):
        s_re, s_im = sens(c)
        u.append(join(s_re * x_re - s_im * x_im, s_re * x_im + s_im * x_re))
    a = jnp.dot(jnp.concatenate(u, axis=0), tables[0], preferred_element_type=F32).astype(BF)
    k = jnp.dot(tables[1], to_deep(a), preferred_element_type=F32)
    m = []
    for c in range(coils):
        k_re, k_im = from_deep(k[:, span * c : span * (c + 1)])
        k_re = keep * (k_re - data_ref[c, :, 0, 0].astype(F32))
        k_im = keep * (k_im - data_ref[c, :, 0, 1].astype(F32))
        m.append(join(k_re, k_im))
    b = jnp.dot(jnp.concatenate(m, axis=0), tables[2], preferred_element_type=F32).astype(BF)
    r = jnp.dot(tables[3], to_deep(b), preferred_element_type=F32)
    acc_re = acc_im = 0.0
    for c in range(coils):
        s_re, s_im = sens(c)
        r_re, r_im = from_deep(r[:, span * c : span * (c + 1)])
        acc_re += s_re * r_re + s_im * r_im
        acc_im += s_re * r_im - s_im * r_re
    total = jnp.concatenate([acc_re, acc_im], axis=1).astype(BF)
    for j in range(steps):

        @pl.when(step == j)
        def _(j=j):
            outs[j][...] = total


def coil_gradient(images, places, coil, sens, data, mask, room, weight=1):
    coils = sens.shape[0]
    rows = (HALF, 2 * NZ, NY)
    steps = len(images)
    (far, low), (far_next, low_next) = places[0], places[-1]

    def place(i, coil):
        return ((coil[0] + far + i * (far_next - far)) & 3) * 2 + low + i * (low_next - low)

    return pl.pallas_call(
        grad_kernel,
        grid_spec=pltpu.PrefetchScalarGridSpec(
            num_scalar_prefetch=1,
            grid=(steps,),
            in_specs=[pl.BlockSpec(rows, lambda i, o, block=block: (block, 0, 0)) for _, block in images]
            + [
                pl.BlockSpec((coils, HALF, 2, NZ, NY), lambda i, o: (0, place(i, o), 0, 0, 0)),
                pl.BlockSpec((coils, HALF, 1, 2, NZ, NY), lambda i, o: (0, place(i, o), 0, 0, 0, 0)),
                pl.BlockSpec((1, NZ, NY), lambda i, o: (0, 0, 0)),
            ]
            + [pl.BlockSpec((4, 256, 256), lambda i, o: (0, 0, 0))],
            out_specs=[pl.BlockSpec(rows, lambda i, o: (0, 0, 0))] * steps,
        ),
        out_shape=[jax.ShapeDtypeStruct(rows, BF)] * steps,
        cost_estimate=pl.CostEstimate(
            flops=weight * steps * HALF * coils * 32 * 2**20,
            bytes_accessed=steps * HALF * coils * 40000,
            transcendentals=0,
        ),
        compiler_params=pltpu.CompilerParams(vmem_limit_bytes=room * 2**20),
        name="coil_gradient",
    )(
        coil, *(x for x, _ in images), sens, data, mask,
        np.stack([wide_table(-1.0), deep_table(-1.0), wide_table(1.0), deep_table(1.0)]),
    )


SMALL = pltpu.CompilerParams(vmem_limit_bytes=8 * 2**20)


def total_of(refs):
    return sum(ref[...].astype(F32) for ref in refs).astype(BF)


def pair_kernel(a, b, out):
    out[...] = total_of((a, b))


def pair_sum(a, b):
    return pl.pallas_call(
        pair_kernel, out_shape=jax.ShapeDtypeStruct(a.shape, BF), compiler_params=SMALL, name="pair_sum",
    )(a, b)


def join_kernel(a0, b0, c0, a1, b1, c1, out_ref):
    out_ref[:HALF] = total_of((a0, b0, c0))
    out_ref[HALF:] = total_of((a1, b1, c1))


def join_sums(first, second):
    return pl.pallas_call(
        join_kernel, out_shape=jax.ShapeDtypeStruct((2 * HALF, 2 * NZ, NY), BF),
        compiler_params=SMALL, name="join_sums",
    )(*first, *second)


def gram_kernel(g_ref, gt_ref, q_ref):
    total = jnp.zeros((2 * FRAMES, 2 * FRAMES), F32)
    for z in range(0, NZ, 16):
        parts = [g_ref[:, pl.ds(p * NZ + z, 16), :].astype(F32) for p in range(2)]
        blocks = jnp.concatenate([jnp.swapaxes(x, 0, 1) for x in parts], axis=1).astype(BF)
        gt_ref[pl.ds(z, 16)] = blocks
        for d in range(0, 16, 2):
            both = jnp.concatenate([blocks[d], blocks[d + 1]], axis=1)
            total += lax.dot_general(both, both, (((1,), (1,)), ((), ())), preferred_element_type=F32)
    h_re = total[:FRAMES, :FRAMES] + total[FRAMES:, FRAMES:]
    h_im = total[:FRAMES, FRAMES:] - total[FRAMES:, :FRAMES]
    row = lax.broadcasted_iota(jnp.int32, (FRAMES, FRAMES), 0)
    col = lax.broadcasted_iota(jnp.int32, (FRAMES, FRAMES), 1)
    q = jnp.where(row <= col, h_re, h_im)
    q_ref[...] = jnp.concatenate([q[8 * j : 8 * j + 8] for j in range(4)], axis=1)


def gram(g):
    return pl.pallas_call(
        gram_kernel,
        out_shape=(
            jax.ShapeDtypeStruct((NZ, 2 * FRAMES, NY), BF),
            jax.ShapeDtypeStruct((8, 128), F32),
        ),
        compiler_params=pltpu.CompilerParams(vmem_limit_bytes=32 * 2**20),
        name="gram",
    )(g)


def exact(a, b, dims=((1,), (0,))):
    return lax.dot_general(
        a, b, (dims, ((), ())), precision=lax.Precision.HIGHEST, preferred_element_type=F32
    )


def final_kernel(q0, q1, q2, q3, start_ref, gt_ref, image_ref, out_ref, spec_ref):
    packed = (q0[...] + q1[...]) + (q2[...] + q3[...])
    q = jnp.concatenate([packed[:, 32 * j : 32 * j + 32] for j in range(4)], axis=0)
    qt = q.T
    row = lax.broadcasted_iota(jnp.int32, (FRAMES, FRAMES), 0)
    col = lax.broadcasted_iota(jnp.int32, (FRAMES, FRAMES), 1)
    h_re = jnp.where(row <= col, q, qt)
    h_im = jnp.where(row > col, q, jnp.where(row < col, -qt, 0.0))
    h = jnp.concatenate(
        [jnp.concatenate([h_re, -h_im], axis=1), jnp.concatenate([h_im, h_re], axis=1)], axis=0
    )
    w = exact(h, jnp.concatenate([start_ref[0], start_ref[1]], axis=0))
    v = w / jnp.sqrt(jnp.sum(w * w, axis=0, keepdims=True) + EPSILON)
    w = exact(h, v)
    power = jnp.maximum(jnp.sum(v * w, axis=0, keepdims=True), 0.0)
    last = jnp.sum(w * w, axis=0, keepdims=True)
    spec_ref[...] = jnp.sqrt(last + EPSILON) / jnp.sqrt(power + EPSILON)
    total = jnp.sum(power, axis=1, keepdims=True)
    scale = 0.5 * math.sqrt(NX * NY * NZ * FRAMES) / jnp.sqrt(total)
    t = exact(v, v, ((1,), (1,)))
    t_re = (t[:FRAMES, :FRAMES] + t[FRAMES:, FRAMES:]) * scale
    t_im = (t[FRAMES:, :FRAMES] - t[:FRAMES, FRAMES:]) * scale
    left = jnp.concatenate(
        [jnp.concatenate([t_re, t_im], axis=1), jnp.concatenate([-t_im, t_re], axis=1)], axis=0
    )
    high = left.astype(BF)
    low = (left - high.astype(F32)).astype(BF)
    left = jnp.concatenate([high, low], axis=1)
    for z in range(0, NZ, 8):
        update = []
        for d in range(z, z + 8, 2):
            both = jnp.concatenate([gt_ref[d], gt_ref[d + 1]], axis=1)
            both = jnp.dot(left, jnp.concatenate([both, both], axis=0), preferred_element_type=F32)
            update += [both[:, :NY], both[:, NY:]]
        update = jnp.swapaxes(jnp.stack(update, axis=0), 0, 1)
        for p in range(2):
            rows = pl.ds(p * NZ + z, 8)
            out_ref[:, rows, :] = 0.5 * image_ref[:, rows, :] - update[p * FRAMES : (p + 1) * FRAMES]


def finish(parts, start, gt, image):
    return pl.pallas_call(
        final_kernel,
        out_shape=(
            jax.ShapeDtypeStruct((FRAMES, 2 * NZ, NY), F32),
            jax.ShapeDtypeStruct((1, start.shape[2]), F32),
        ),
        compiler_params=pltpu.CompilerParams(vmem_limit_bytes=32 * 2**20),
        name="finish",
    )(*parts, start, gt, image)


RIGHT = [(i, (i + 1) % 4) for i in range(4)]
LEFT = [(i, (i + 3) % 4) for i in range(4)]


def after(x, *others):
    return lax.optimization_barrier((x,) + others)[0]


def local(image, sens, data, mask, start):
    flat = image.reshape(FRAMES, 2 * NZ, NY)
    coil = lax.axis_index("coil").astype(jnp.int32).reshape(1)

    def partial(images, places, *others, room=28):
        return coil_gradient(images, places, after(coil, *others), sens, data, mask, room)

    def right(x):
        return lax.ppermute(x, "coil", RIGHT)

    def left(x):
        return lax.ppermute(x, "coil", LEFT)

    own = lax.all_to_all(flat.astype(BF), "frame", split_axis=0, concat_axis=0, tiled=True)
    own0, own1 = own[:HALF], own[HALF:]
    left0, right1 = right(own0), left(own1)
    rows = [lax.dynamic_slice_in_dim(x, coil[0] * 2 * HALF, 2 * HALF, axis=1) for x in (sens, data)]
    g_own0, g_own1 = coil_gradient(
        [(own, 0), (own, 1)], [(0, 0), (0, 1)], jnp.zeros_like(coil), *rows, mask, 28, 2
    )
    left0, right1 = after(left0, g_own1, right1), after(right1, g_own1, left0)
    far0, far1 = right(left0), left(right1)
    g_left0, g_right1 = partial([(left0, 0), (right1, 0)], [(3, 0), (1, 1)])
    left1, right0 = right(after(own1, g_left0)), left(after(own0, g_left0))
    (g_far0,) = partial([(far0, 0)], [(2, 0)], g_left0)
    (g_far1,) = partial([(far1, 0)], [(2, 1)], g_far0)
    low, high = right(g_far0), left(g_far1)
    in_left1, in_right0 = right(after(g_right1, g_far1)), left(after(g_left0, g_far1))
    g_left1, g_right0 = partial([(left1, 0), (right0, 0)], [(3, 1), (1, 0)], g_far1)
    in_left0, in_right1 = right(pair_sum(g_right0, low)), left(pair_sum(g_left1, high))
    gradient = join_sums((g_own0, in_left0, in_right0), (g_own1, in_left1, in_right1))
    frames = lax.all_to_all(gradient, "frame", split_axis=0, concat_axis=0, tiled=True)
    gt, q = gram(frames)
    spread = lax.all_to_all(
        jnp.broadcast_to(q[None], (FRAMES, 8, 128)), "frame", split_axis=0, concat_axis=0, tiled=True
    )
    q = jnp.sum(spread, axis=0)
    parts = [q] + [lax.ppermute(q, "coil", [(i, i ^ d) for i in range(4)]) for d in (1, 2, 3)]
    new_image, spectrum = finish(parts, start, gt, flat)
    return new_image.reshape(image.shape), spectrum[0]


def solution(mesh):
    return jax.shard_map(
        local,
        mesh=mesh,
        in_specs=(
            P(("coil", "frame"), None, None, None, None),
            P("coil", None, None, None, None),
            P("coil", None, "frame", None, None, None),
            P("frame", None, None),
            P(),
        ),
        out_specs=(P(("coil", "frame"), None, None, None, None), P()),
        check_vma=False,
    )
```

```python
import math

import jax
import jax.numpy as jnp
import ml_dtypes
import numpy as np
from jax import lax
from jax.experimental import pallas as pl
from jax.experimental.pallas import tpu as pltpu
from jax.sharding import PartitionSpec as P

NX = 128
NY = 128
NZ = 32
FRAMES = 32
HALF = 16
EPSILON = 1e-06
BF = jnp.bfloat16
F32 = jnp.float32


def dft_tables(length):
    counter = np.arange(length)
    product = counter[:, None] * counter[None, :] % length
    angles = product.astype(np.float32) * np.float32(2.0 * math.pi / length)
    factor = np.float32(1.0 / math.sqrt(length))
    return np.cos(angles) * factor, np.sin(angles) * factor


def wide_table(sign):
    c, s = dft_tables(NY)
    return np.block([[c, sign * s], [-sign * s, c]]).astype(ml_dtypes.bfloat16)


def deep_table(sign):
    c, s = dft_tables(NZ)
    one = np.block([[c, -sign * s], [sign * s, c]])
    return np.kron(np.eye(4, dtype=np.float32), one).astype(ml_dtypes.bfloat16)


def to_deep(a):
    out = []
    for j in range(0, a.shape[0], 256):
        one = a[j : j + 256].reshape(8, NZ, 2 * NY)
        one = jnp.concatenate([one[:, :, :NY], one[:, :, NY:]], axis=1).reshape(512, NY)
        out += [one[:256], one[256:]]
    return jnp.concatenate(out, axis=1)


def from_deep(k):
    k = jnp.concatenate([k[:, j : j + NY] for j in range(0, k.shape[1], NY)], axis=0)
    k = k.reshape(-1, 2 * NZ, NY)
    return k[:, :NZ], k[:, NZ:]


def grad_kernel(coil_ref, *refs):
    steps = (len(refs) - 4) // 2
    images, refs = refs[:steps], refs[steps:]
    sens_ref, data_ref, mask_ref, tables = refs[:4]
    outs = refs[4:]
    step = pl.program_id(0)
    coils = sens_ref.shape[0]
    span = HALF * NZ
    img = images[0][...]
    if steps == 2:
        img = jnp.where(step == 0, img, images[1][...])
    img = img.astype(F32)
    x_re, x_im = img[:, :NZ], img[:, NZ:]
    keep = mask_ref[0].astype(F32)[None]

    def sens(c):
        return sens_ref[c, :, 0].astype(F32), sens_ref[c, :, 1].astype(F32)

    def join(re, im):
        return jnp.concatenate([re, im], axis=-1).astype(BF).reshape(span, 2 * NY)

    u = []
    for c in range(coils):
        s_re, s_im = sens(c)
        u.append(join(s_re * x_re - s_im * x_im, s_re * x_im + s_im * x_re))
    a = jnp.dot(jnp.concatenate(u, axis=0), tables[0], preferred_element_type=F32).astype(BF)
    k = jnp.dot(tables[1], to_deep(a), preferred_element_type=F32)
    m = []
    for c in range(coils):
        k_re, k_im = from_deep(k[:, span * c : span * (c + 1)])
        k_re = keep * (k_re - data_ref[c, :, 0, 0].astype(F32))
        k_im = keep * (k_im - data_ref[c, :, 0, 1].astype(F32))
        m.append(join(k_re, k_im))
    b = jnp.dot(jnp.concatenate(m, axis=0), tables[2], preferred_element_type=F32).astype(BF)
    r = jnp.dot(tables[3], to_deep(b), preferred_element_type=F32)
    acc_re = acc_im = 0.0
    for c in range(coils):
        s_re, s_im = sens(c)
        r_re, r_im = from_deep(r[:, span * c : span * (c + 1)])
        acc_re += s_re * r_re + s_im * r_im
        acc_im += s_re * r_im - s_im * r_re
    total = jnp.concatenate([acc_re, acc_im], axis=1).astype(BF)
    for j in range(steps):

        @pl.when(step == j)
        def _(j=j):
            outs[j][...] = total


def coil_gradient(images, places, coil, sens, data, mask, room, weight=1):
    coils = sens.shape[0]
    rows = (HALF, 2 * NZ, NY)
    steps = len(images)
    (far, low), (far_next, low_next) = places[0], places[-1]

    def place(i, coil):
        return ((coil[0] + far + i * (far_next - far)) & 3) * 2 + low + i * (low_next - low)

    return pl.pallas_call(
        grad_kernel,
        grid_spec=pltpu.PrefetchScalarGridSpec(
            num_scalar_prefetch=1,
            grid=(steps,),
            in_specs=[pl.BlockSpec(rows, lambda i, o, block=block: (block, 0, 0)) for _, block in images]
            + [
                pl.BlockSpec((coils, HALF, 2, NZ, NY), lambda i, o: (0, place(i, o), 0, 0, 0)),
                pl.BlockSpec((coils, HALF, 1, 2, NZ, NY), lambda i, o: (0, place(i, o), 0, 0, 0, 0)),
                pl.BlockSpec((1, NZ, NY), lambda i, o: (0, 0, 0)),
            ]
            + [pl.BlockSpec((4, 256, 256), lambda i, o: (0, 0, 0))],
            out_specs=[pl.BlockSpec(rows, lambda i, o: (0, 0, 0))] * steps,
        ),
        out_shape=[jax.ShapeDtypeStruct(rows, BF)] * steps,
        cost_estimate=pl.CostEstimate(
            flops=weight * steps * HALF * coils * 32 * 2**20,
            bytes_accessed=steps * HALF * coils * 40000,
            transcendentals=0,
        ),
        compiler_params=pltpu.CompilerParams(vmem_limit_bytes=room * 2**20),
        name="coil_gradient",
    )(
        coil, *(x for x, _ in images), sens, data, mask,
        np.stack([wide_table(-1.0), deep_table(-1.0), wide_table(1.0), deep_table(1.0)]),
    )


SMALL = pltpu.CompilerParams(vmem_limit_bytes=8 * 2**20)


def total_of(refs):
    return sum(ref[...].astype(F32) for ref in refs).astype(BF)


def pair_kernel(a, b, out):
    out[...] = total_of((a, b))


def pair_sum(a, b):
    return pl.pallas_call(
        pair_kernel, out_shape=jax.ShapeDtypeStruct(a.shape, BF), compiler_params=SMALL, name="pair_sum",
    )(a, b)


def join_kernel(a0, b0, c0, a1, b1, c1, out_ref):
    out_ref[:HALF] = total_of((a0, b0, c0))
    out_ref[HALF:] = total_of((a1, b1, c1))


def join_sums(first, second):
    return pl.pallas_call(
        join_kernel, out_shape=jax.ShapeDtypeStruct((2 * HALF, 2 * NZ, NY), BF),
        compiler_params=SMALL, name="join_sums",
    )(*first, *second)


def gram_kernel(g_ref, gt_ref, q_ref):
    total = jnp.zeros((2 * FRAMES, 2 * FRAMES), F32)
    for z in range(0, NZ, 16):
        parts = [g_ref[:, pl.ds(p * NZ + z, 16), :].astype(F32) for p in range(2)]
        blocks = jnp.concatenate([jnp.swapaxes(x, 0, 1) for x in parts], axis=1).astype(BF)
        gt_ref[pl.ds(z, 16)] = blocks
        for d in range(0, 16, 2):
            both = jnp.concatenate([blocks[d], blocks[d + 1]], axis=1)
            total += lax.dot_general(both, both, (((1,), (1,)), ((), ())), preferred_element_type=F32)
    h_re = total[:FRAMES, :FRAMES] + total[FRAMES:, FRAMES:]
    h_im = total[:FRAMES, FRAMES:] - total[FRAMES:, :FRAMES]
    row = lax.broadcasted_iota(jnp.int32, (FRAMES, FRAMES), 0)
    col = lax.broadcasted_iota(jnp.int32, (FRAMES, FRAMES), 1)
    q = jnp.where(row <= col, h_re, h_im)
    q_ref[...] = jnp.concatenate([q[8 * j : 8 * j + 8] for j in range(4)], axis=1)


def gram(g):
    return pl.pallas_call(
        gram_kernel,
        out_shape=(
            jax.ShapeDtypeStruct((NZ, 2 * FRAMES, NY), BF),
            jax.ShapeDtypeStruct((8, 128), F32),
        ),
        compiler_params=pltpu.CompilerParams(vmem_limit_bytes=32 * 2**20),
        name="gram",
    )(g)


def exact(a, b, dims=((1,), (0,))):
    return lax.dot_general(
        a, b, (dims, ((), ())), precision=lax.Precision.HIGHEST, preferred_element_type=F32
    )


def final_kernel(q0, q1, q2, q3, start_ref, gt_ref, image_ref, out_ref, spec_ref):
    packed = (q0[...] + q2[...]) + (q1[...] + q3[...])
    q = jnp.concatenate([packed[:, 32 * j : 32 * j + 32] for j in range(4)], axis=0)
    qt = q.T
    row = lax.broadcasted_iota(jnp.int32, (FRAMES, FRAMES), 0)
    col = lax.broadcasted_iota(jnp.int32, (FRAMES, FRAMES), 1)
    h_re = jnp.where(row <= col, q, qt)
    h_im = jnp.where(row > col, q, jnp.where(row < col, -qt, 0.0))
    h = jnp.concatenate(
        [jnp.concatenate([h_re, -h_im], axis=1), jnp.concatenate([h_im, h_re], axis=1)], axis=0
    )
    w = exact(h, jnp.concatenate([start_ref[0], start_ref[1]], axis=0))
    v = w / jnp.sqrt(jnp.sum(w * w, axis=0, keepdims=True) + EPSILON)
    w = exact(h, v)
    power = jnp.maximum(jnp.sum(v * w, axis=0, keepdims=True), 0.0)
    last = jnp.sum(w * w, axis=0, keepdims=True)
    spec_ref[...] = jnp.sqrt(last + EPSILON) / jnp.sqrt(power + EPSILON)
    total = jnp.sum(power, axis=1, keepdims=True)
    scale = 0.5 * math.sqrt(NX * NY * NZ * FRAMES) / jnp.sqrt(total)
    t = exact(v, v, ((1,), (1,)))
    t_re = (t[:FRAMES, :FRAMES] + t[FRAMES:, FRAMES:]) * scale
    t_im = (t[FRAMES:, :FRAMES] - t[:FRAMES, FRAMES:]) * scale
    left = jnp.concatenate(
        [jnp.concatenate([t_re, t_im], axis=1), jnp.concatenate([-t_im, t_re], axis=1)], axis=0
    )
    high = left.astype(BF)
    low = (left - high.astype(F32)).astype(BF)
    left = jnp.concatenate([high, low], axis=1)
    for z in range(0, NZ, 8):
        update = []
        for d in range(z, z + 8, 2):
            both = jnp.concatenate([gt_ref[d], gt_ref[d + 1]], axis=1)
            both = jnp.dot(left, jnp.concatenate([both, both], axis=0), preferred_element_type=F32)
            update += [both[:, :NY], both[:, NY:]]
        update = jnp.swapaxes(jnp.stack(update, axis=0), 0, 1)
        for p in range(2):
            rows = pl.ds(p * NZ + z, 8)
            out_ref[:, rows, :] = 0.5 * image_ref[:, rows, :] - update[p * FRAMES : (p + 1) * FRAMES]


def finish(parts, start, gt, image):
    return pl.pallas_call(
        final_kernel,
        out_shape=(
            jax.ShapeDtypeStruct((FRAMES, 2 * NZ, NY), F32),
            jax.ShapeDtypeStruct((1, start.shape[2]), F32),
        ),
        compiler_params=pltpu.CompilerParams(vmem_limit_bytes=32 * 2**20),
        name="finish",
    )(*parts, start, gt, image)


RIGHT = [(i, (i + 1) % 4) for i in range(4)]
LEFT = [(i, (i + 3) % 4) for i in range(4)]


def after(x, *others):
    return lax.optimization_barrier((x,) + others)[0]


def local(image, sens, data, mask, start):
    flat = image.reshape(FRAMES, 2 * NZ, NY)
    coil = lax.axis_index("coil").astype(jnp.int32).reshape(1)

    def partial(images, places, *others, room=28):
        return coil_gradient(images, places, after(coil, *others), sens, data, mask, room)

    def right(x):
        return lax.ppermute(x, "coil", RIGHT)

    def left(x):
        return lax.ppermute(x, "coil", LEFT)

    own = lax.all_to_all(flat.astype(BF), "frame", split_axis=0, concat_axis=0, tiled=True)
    own0, own1 = own[:HALF], own[HALF:]
    left0, right1 = right(own0), left(own1)
    rows = [lax.dynamic_slice_in_dim(x, coil[0] * 2 * HALF, 2 * HALF, axis=1) for x in (sens, data)]
    g_own0, g_own1 = coil_gradient(
        [(own, 0), (own, 1)], [(0, 0), (0, 1)], jnp.zeros_like(coil), *rows, mask, 28, 2
    )
    left0, right1 = after(left0, g_own1, right1), after(right1, g_own1, left0)
    far0, far1 = right(left0), left(right1)
    g_left0, g_right1 = partial([(left0, 0), (right1, 0)], [(3, 0), (1, 1)])
    left1, right0 = right(after(own1, g_left0)), left(after(own0, g_left0))
    (g_far0,) = partial([(far0, 0)], [(2, 0)], g_left0)
    (g_far1,) = partial([(far1, 0)], [(2, 1)], g_far0)
    low, high = right(g_far0), left(g_far1)
    in_left1, in_right0 = right(after(g_right1, g_far1)), left(after(g_left0, g_far1))
    g_left1, g_right0 = partial([(left1, 0), (right0, 0)], [(3, 1), (1, 0)], g_far1)
    in_left0, in_right1 = right(pair_sum(g_right0, low)), left(pair_sum(g_left1, high))
    gradient = join_sums((g_own0, in_left0, in_right0), (g_own1, in_left1, in_right1))
    frames = lax.all_to_all(gradient, "frame", split_axis=0, concat_axis=0, tiled=True)
    gt, q = gram(frames)
    spread = lax.all_to_all(
        jnp.broadcast_to(q[None], (FRAMES, 8, 128)), "frame", split_axis=0, concat_axis=0, tiled=True
    )
    q = jnp.sum(spread, axis=0)
    across = lax.ppermute(q, "coil", [(i, i ^ 2) for i in range(4)])
    parts = [q, left(q), across, right(q)]
    new_image, spectrum = finish(parts, start, gt, flat)
    return new_image.reshape(image.shape), spectrum[0]


def solution(mesh):
    return jax.shard_map(
        local,
        mesh=mesh,
        in_specs=(
            P(("coil", "frame"), None, None, None, None),
            P("coil", None, None, None, None),
            P("coil", None, "frame", None, None, None),
            P("frame", None, None),
            P(),
        ),
        out_specs=(P(("coil", "frame"), None, None, None, None), P()),
        check_vma=False,
    )
```

```python
import math

import jax
import jax.numpy as jnp
import ml_dtypes
import numpy as np
from jax import lax
from jax.experimental import pallas as pl
from jax.experimental.pallas import tpu as pltpu
from jax.sharding import PartitionSpec as P

NX = 128
NY = 128
NZ = 32
FRAMES = 32
HALF = 16
EPSILON = 1e-06
BF = jnp.bfloat16
F32 = jnp.float32


def dft_tables(length):
    counter = np.arange(length)
    product = counter[:, None] * counter[None, :] % length
    angles = product.astype(np.float32) * np.float32(2.0 * math.pi / length)
    factor = np.float32(1.0 / math.sqrt(length))
    return np.cos(angles) * factor, np.sin(angles) * factor


def wide_table(sign):
    c, s = dft_tables(NY)
    return np.block([[c, sign * s], [-sign * s, c]]).astype(ml_dtypes.bfloat16)


def deep_table(sign):
    c, s = dft_tables(NZ)
    one = np.block([[c, -sign * s], [sign * s, c]])
    return np.kron(np.eye(4, dtype=np.float32), one).astype(ml_dtypes.bfloat16)


def to_deep(a):
    out = []
    for j in range(0, a.shape[0], 256):
        one = a[j : j + 256].reshape(8, NZ, 2 * NY)
        one = jnp.concatenate([one[:, :, :NY], one[:, :, NY:]], axis=1).reshape(512, NY)
        out += [one[:256], one[256:]]
    return jnp.concatenate(out, axis=1)


def from_deep(k):
    k = jnp.concatenate([k[:, j : j + NY] for j in range(0, k.shape[1], NY)], axis=0)
    k = k.reshape(-1, 2 * NZ, NY)
    return k[:, :NZ], k[:, NZ:]


def grad_kernel(coil_ref, *refs):
    steps = (len(refs) - 4) // 2
    images, refs = refs[:steps], refs[steps:]
    sens_ref, data_ref, mask_ref, tables = refs[:4]
    outs = refs[4:]
    step = pl.program_id(0)
    coils = sens_ref.shape[0]
    span = HALF * NZ
    img = images[0][...]
    if steps == 2:
        img = jnp.where(step == 0, img, images[1][...])
    img = img.astype(F32)
    x_re, x_im = img[:, :NZ], img[:, NZ:]
    keep = mask_ref[0].astype(F32)[None]

    def sens(c):
        return sens_ref[c, :, 0].astype(F32), sens_ref[c, :, 1].astype(F32)

    def join(re, im):
        return jnp.concatenate([re, im], axis=-1).astype(BF).reshape(span, 2 * NY)

    u = []
    for c in range(coils):
        s_re, s_im = sens(c)
        u.append(join(s_re * x_re - s_im * x_im, s_re * x_im + s_im * x_re))
    a = jnp.dot(jnp.concatenate(u, axis=0), tables[0], preferred_element_type=F32).astype(BF)
    k = jnp.dot(tables[1], to_deep(a), preferred_element_type=F32)
    m = []
    for c in range(coils):
        k_re, k_im = from_deep(k[:, span * c : span * (c + 1)])
        k_re = keep * (k_re - data_ref[c, :, 0, 0].astype(F32))
        k_im = keep * (k_im - data_ref[c, :, 0, 1].astype(F32))
        m.append(join(k_re, k_im))
    b = jnp.dot(jnp.concatenate(m, axis=0), tables[2], preferred_element_type=F32).astype(BF)
    r = jnp.dot(tables[3], to_deep(b), preferred_element_type=F32)
    acc_re = acc_im = 0.0
    for c in range(coils):
        s_re, s_im = sens(c)
        r_re, r_im = from_deep(r[:, span * c : span * (c + 1)])
        acc_re += s_re * r_re + s_im * r_im
        acc_im += s_re * r_im - s_im * r_re
    total = jnp.concatenate([acc_re, acc_im], axis=1).astype(BF)
    for j in range(steps):

        @pl.when(step == j)
        def _(j=j):
            outs[j][...] = total


def coil_gradient(images, places, coil, sens, data, mask, room, weight=1):
    coils = sens.shape[0]
    rows = (HALF, 2 * NZ, NY)
    steps = len(images)
    (far, low), (far_next, low_next) = places[0], places[-1]

    def place(i, coil):
        return ((coil[0] + far + i * (far_next - far)) & 3) * 2 + low + i * (low_next - low)

    return pl.pallas_call(
        grad_kernel,
        grid_spec=pltpu.PrefetchScalarGridSpec(
            num_scalar_prefetch=1,
            grid=(steps,),
            in_specs=[pl.BlockSpec(rows, lambda i, o, block=block: (block, 0, 0)) for _, block in images]
            + [
                pl.BlockSpec((coils, HALF, 2, NZ, NY), lambda i, o: (0, place(i, o), 0, 0, 0)),
                pl.BlockSpec((coils, HALF, 1, 2, NZ, NY), lambda i, o: (0, place(i, o), 0, 0, 0, 0)),
                pl.BlockSpec((1, NZ, NY), lambda i, o: (0, 0, 0)),
            ]
            + [pl.BlockSpec((4, 256, 256), lambda i, o: (0, 0, 0))],
            out_specs=[pl.BlockSpec(rows, lambda i, o: (0, 0, 0))] * steps,
        ),
        out_shape=[jax.ShapeDtypeStruct(rows, BF)] * steps,
        cost_estimate=pl.CostEstimate(
            flops=weight * steps * HALF * coils * 32 * 2**20,
            bytes_accessed=steps * HALF * coils * 40000,
            transcendentals=0,
        ),
        compiler_params=pltpu.CompilerParams(vmem_limit_bytes=room * 2**20),
        name="coil_gradient",
    )(
        coil, *(x for x, _ in images), sens, data, mask,
        np.stack([wide_table(-1.0), deep_table(-1.0), wide_table(1.0), deep_table(1.0)]),
    )


SMALL = pltpu.CompilerParams(vmem_limit_bytes=8 * 2**20)


def total_of(refs):
    return sum(ref[...].astype(F32) for ref in refs).astype(BF)


def pair_kernel(a, b, out):
    out[...] = total_of((a, b))


def pair_sum(a, b):
    return pl.pallas_call(
        pair_kernel, out_shape=jax.ShapeDtypeStruct(a.shape, BF), compiler_params=SMALL, name="pair_sum",
    )(a, b)


def join_kernel(a0, b0, c0, a1, b1, c1, out_ref):
    out_ref[:HALF] = total_of((a0, b0, c0))
    out_ref[HALF:] = total_of((a1, b1, c1))


def join_sums(first, second):
    return pl.pallas_call(
        join_kernel, out_shape=jax.ShapeDtypeStruct((2 * HALF, 2 * NZ, NY), BF),
        compiler_params=SMALL, name="join_sums",
    )(*first, *second)


def gram_kernel(g_ref, gt_ref, q_ref):
    total = jnp.zeros((2 * FRAMES, 2 * FRAMES), F32)
    for z in range(0, NZ, 16):
        parts = [g_ref[:, pl.ds(p * NZ + z, 16), :].astype(F32) for p in range(2)]
        blocks = jnp.concatenate([jnp.swapaxes(x, 0, 1) for x in parts], axis=1).astype(BF)
        gt_ref[pl.ds(z, 16)] = blocks
        for d in range(0, 16, 2):
            both = jnp.concatenate([blocks[d], blocks[d + 1]], axis=1)
            total += lax.dot_general(both, both, (((1,), (1,)), ((), ())), preferred_element_type=F32)
    h_re = total[:FRAMES, :FRAMES] + total[FRAMES:, FRAMES:]
    h_im = total[:FRAMES, FRAMES:] - total[FRAMES:, :FRAMES]
    row = lax.broadcasted_iota(jnp.int32, (FRAMES, FRAMES), 0)
    col = lax.broadcasted_iota(jnp.int32, (FRAMES, FRAMES), 1)
    q = jnp.where(row <= col, h_re, h_im)
    q_ref[...] = jnp.concatenate([q[8 * j : 8 * j + 8] for j in range(4)], axis=1)


def gram(g):
    return pl.pallas_call(
        gram_kernel,
        out_shape=(
            jax.ShapeDtypeStruct((NZ, 2 * FRAMES, NY), BF),
            jax.ShapeDtypeStruct((8, 128), F32),
        ),
        compiler_params=pltpu.CompilerParams(vmem_limit_bytes=32 * 2**20),
        name="gram",
    )(g)


def exact(a, b, dims=((1,), (0,))):
    return lax.dot_general(
        a, b, (dims, ((), ())), precision=lax.Precision.HIGHEST, preferred_element_type=F32
    )


def final_kernel(q0, q1, q2, q3, start_ref, gt_ref, image_ref, out_ref, spec_ref, done, sems):
    packed = (q0[...] + q2[...]) + (q1[...] + q3[...])
    q = jnp.concatenate([packed[:, 32 * j : 32 * j + 32] for j in range(4)], axis=0)
    qt = q.T
    row = lax.broadcasted_iota(jnp.int32, (FRAMES, FRAMES), 0)
    col = lax.broadcasted_iota(jnp.int32, (FRAMES, FRAMES), 1)
    h_re = jnp.where(row <= col, q, qt)
    h_im = jnp.where(row > col, q, jnp.where(row < col, -qt, 0.0))
    h = jnp.concatenate(
        [jnp.concatenate([h_re, -h_im], axis=1), jnp.concatenate([h_im, h_re], axis=1)], axis=0
    )
    w = exact(h, jnp.concatenate([start_ref[0], start_ref[1]], axis=0))
    v = w / jnp.sqrt(jnp.sum(w * w, axis=0, keepdims=True) + EPSILON)
    w = exact(h, v)
    power = jnp.maximum(jnp.sum(v * w, axis=0, keepdims=True), 0.0)
    last = jnp.sum(w * w, axis=0, keepdims=True)
    spec_ref[...] = jnp.sqrt(last + EPSILON) / jnp.sqrt(power + EPSILON)
    total = jnp.sum(power, axis=1, keepdims=True)
    scale = 0.5 * math.sqrt(NX * NY * NZ * FRAMES) / jnp.sqrt(total)
    t = exact(v, v, ((1,), (1,)))
    t_re = (t[:FRAMES, :FRAMES] + t[FRAMES:, FRAMES:]) * scale
    t_im = (t[FRAMES:, :FRAMES] - t[:FRAMES, FRAMES:]) * scale
    left = jnp.concatenate(
        [jnp.concatenate([t_re, t_im], axis=1), jnp.concatenate([-t_im, t_re], axis=1)], axis=0
    )
    high = left.astype(BF)
    low = (left - high.astype(F32)).astype(BF)
    left = jnp.concatenate([high, low], axis=1)
    copies = []
    for z in range(0, NZ, 8):
        update = []
        for d in range(z, z + 8, 2):
            both = jnp.concatenate([gt_ref[d], gt_ref[d + 1]], axis=1)
            both = jnp.dot(left, jnp.concatenate([both, both], axis=0), preferred_element_type=F32)
            update += [both[:, :NY], both[:, NY:]]
        update = jnp.swapaxes(jnp.stack(update, axis=0), 0, 1)
        for p in range(2):
            rows = pl.ds(p * NZ + z, 8)
            done[:, rows, :] = 0.5 * image_ref[:, rows, :] - update[p * FRAMES : (p + 1) * FRAMES]
            copies.append(
                pltpu.make_async_copy(done.at[:, rows, :], out_ref.at[:, rows, :], sems.at[p, z // 8])
            )
            copies[-1].start()
    for copy in copies:
        copy.wait()


def finish(parts, start, gt, image):
    return pl.pallas_call(
        final_kernel,
        out_shape=(
            jax.ShapeDtypeStruct((FRAMES, 2 * NZ, NY), F32),
            jax.ShapeDtypeStruct((1, start.shape[2]), F32),
        ),
        out_specs=(pl.BlockSpec(memory_space=pl.ANY), pl.BlockSpec(memory_space=pltpu.VMEM)),
        scratch_shapes=[
            pltpu.VMEM((FRAMES, 2 * NZ, NY), F32),
            pltpu.SemaphoreType.DMA((2, NZ // 8)),
        ],
        compiler_params=pltpu.CompilerParams(vmem_limit_bytes=32 * 2**20),
        name="finish",
    )(*parts, start, gt, image)


RIGHT = [(i, (i + 1) % 4) for i in range(4)]
LEFT = [(i, (i + 3) % 4) for i in range(4)]


def after(x, *others):
    return lax.optimization_barrier((x,) + others)[0]


def local(image, sens, data, mask, start):
    flat = image.reshape(FRAMES, 2 * NZ, NY)
    coil = lax.axis_index("coil").astype(jnp.int32).reshape(1)

    def partial(images, places, *others, room=28):
        return coil_gradient(images, places, after(coil, *others), sens, data, mask, room)

    def right(x):
        return lax.ppermute(x, "coil", RIGHT)

    def left(x):
        return lax.ppermute(x, "coil", LEFT)

    own = lax.all_to_all(flat.astype(BF), "frame", split_axis=0, concat_axis=0, tiled=True)
    own0, own1 = own[:HALF], own[HALF:]
    left0, right1 = right(own0), left(own1)
    rows = [lax.dynamic_slice_in_dim(x, coil[0] * 2 * HALF, 2 * HALF, axis=1) for x in (sens, data)]
    g_own0, g_own1 = coil_gradient(
        [(own, 0), (own, 1)], [(0, 0), (0, 1)], jnp.zeros_like(coil), *rows, mask, 28, 2
    )
    left0, right1 = after(left0, g_own1, right1), after(right1, g_own1, left0)
    far0, far1 = right(left0), left(right1)
    g_left0, g_right1 = partial([(left0, 0), (right1, 0)], [(3, 0), (1, 1)])
    left1, right0 = right(after(own1, g_left0)), left(after(own0, g_left0))
    (g_far0,) = partial([(far0, 0)], [(2, 0)], g_left0)
    (g_far1,) = partial([(far1, 0)], [(2, 1)], g_far0)
    low, high = right(g_far0), left(g_far1)
    in_left1, in_right0 = right(after(g_right1, g_far1)), left(after(g_left0, g_far1))
    g_left1, g_right0 = partial([(left1, 0), (right0, 0)], [(3, 1), (1, 0)], g_far1)
    in_left0, in_right1 = right(pair_sum(g_right0, low)), left(pair_sum(g_left1, high))
    gradient = join_sums((g_own0, in_left0, in_right0), (g_own1, in_left1, in_right1))
    frames = lax.all_to_all(gradient, "frame", split_axis=0, concat_axis=0, tiled=True)
    gt, q = gram(frames)
    spread = lax.all_to_all(
        jnp.broadcast_to(q[None], (FRAMES, 8, 128)), "frame", split_axis=0, concat_axis=0, tiled=True
    )
    q = jnp.sum(spread, axis=0)
    across = lax.ppermute(q, "coil", [(i, i ^ 2) for i in range(4)])
    parts = [q, left(q), across, right(q)]
    new_image, spectrum = finish(parts, start, gt, flat)
    return new_image.reshape(image.shape), spectrum[0]


def solution(mesh):
    return jax.shard_map(
        local,
        mesh=mesh,
        in_specs=(
            P(("coil", "frame"), None, None, None, None),
            P("coil", None, None, None, None),
            P("coil", None, "frame", None, None, None),
            P("frame", None, None),
            P(),
        ),
        out_specs=(P(("coil", "frame"), None, None, None, None), P()),
        check_vma=False,
    )
```
